32 devices in a mesh: dp: 8 (over z, y), seq: 4 (over x, core).
Axes of the slice: x: 2, y: 2, z: 4, core: 2. Of those that a mesh axis runs over, the one named last changes fastest.
Arguments:
- tokens: bfloat16 [8, 1536, 896], P('dp', 'seq'), may hold values from -6 to 6
- doc_lengths: int32 [8, 5], P('dp'), may hold values from 96 to 960, as said below
- cotangent: bfloat16 [8, 1536, 896], P('dp', 'seq'), may hold values from -6 to 6
- norm_one: bfloat16 [896], P('seq'), may hold values from 0.5 to 1.5
- w_qkv: bfloat16 [896, 1152], P('seq'), may hold values from -0.1875 to 0.1875
- b_qkv: bfloat16 [1152], P('seq'), may hold values from -3 to 3
- w_out: bfloat16 [896, 896], P('seq'), may hold values from -1.5 to 1.5
- norm_two: bfloat16 [896], P('seq'), may hold values from 0.5 to 1.5
- w_gate: bfloat16 [896, 4864], P('seq'), may hold values from -0.1875 to 0.1875
- w_up: bfloat16 [896, 4864], P('seq'), may hold values from -0.1875 to 0.1875
- w_down: bfloat16 [4864, 896], P('seq'), may hold values from -0.078125 to 0.078125
Outputs:
- layer_out: bfloat16 [8, 1536, 896], P('dp', 'seq')
- grad_tokens: float32 [8, 1536, 896], P('dp', 'seq')
- grad_norm_one: float32 [896], P('seq')
- grad_w_qkv: float32 [896, 1152], P('seq')
- grad_b_qkv: float32 [1152], P('seq')
- grad_w_out: float32 [896, 896], P('seq')
- grad_norm_two: float32 [896], P('seq')
- grad_w_gate: float32 [896, 4864], P('seq')
- grad_w_up: float32 [896, 4864], P('seq')
- grad_w_down: float32 [4864, 896], P('seq')
The draws below stay inside these ranges and needn't reach their ends.
Inputs may be any that keep to these rules, and one draw needn't show every extreme that they name: `doc_lengths`: each row packs 5 documents in order: the first two together hold 3 * (96) tokens, each between 96 and 192; the third holds 960; the fourth 384 // 4 and the fifth 384 // 2.
All inputs are finite; a program needn't handle non-finite values.
Results may differ from the reference program's by a relative error of at most 0.02.
Values may be sent and summed in bfloat16 or wider, within the bound.
No kernel may reach another device: no remote copies, remote signals or barrier semaphores. Data moves between devices by JAX's collectives and lax.ppermute only.
A program may use at most 192 MiB of HBM per device.

```python
import math
import jax
import jax.numpy as jnp
from jax import lax

D = 896
HEADS = 14
KV_HEADS = 2
HEAD_DIM = 64
FF = 4864
TOK_DEV = 384
QKV = 1152
LENGTH = 1536
SEQS = 8


def draw_doc_lengths(key, part):
    key = jax.random.fold_in(key, 7)
    quarter = TOK_DEV // 4
    split = jax.random.randint(key, (SEQS, 1), quarter, 2 * quarter + 1).astype(jnp.int32)
    second = (3 * quarter - split).astype(jnp.int32)
    middle = jnp.full((SEQS, 1), LENGTH - 6 * quarter, jnp.int32)
    fourth = jnp.full((SEQS, 1), quarter, jnp.int32)
    fifth = jnp.full((SEQS, 1), 2 * quarter, jnp.int32)
    return jnp.concatenate([split, second, middle, fourth, fifth], axis=1).astype(jnp.int32)


def shard_levels(stream_key, dims, shards, smallest, top_value):
    level, own = 1.0, jax.random.fold_in(stream_key, 6)
    for position, parts in shards:
        heights = jnp.exp(jax.random.uniform(jax.random.fold_in(own, position), (parts,), jnp.float32, smallest / len(shards), top_value / len(shards)))
        level = level * jnp.repeat(heights, dims[position] // parts).reshape([-1 if axis == position else 1 for axis in range(len(dims))])
    return level


def scatter_about(rng, dims, scale, bound, cuts=(), held_as=jnp.bfloat16):
    values = scale * jax.random.normal(rng, dims, jnp.float32)
    if cuts:
        values = values * shard_levels(rng, dims, cuts, -0.22, 0.18)
    return jnp.clip(values, -bound, bound).astype(held_as)


def setup_inputs(seed: int = 0) -> dict:
    seeds = jax.random.split(jax.random.key(seed), 12)
    return {
        "tokens": scatter_about(seeds[0], (SEQS, LENGTH, D), 1.0, 6.0, ((0, 8), (1, 4))),
        "doc_lengths": draw_doc_lengths(jax.random.fold_in(seeds[11], 71), 0),
        "cotangent": scatter_about(seeds[2], (SEQS, LENGTH, D), 1.0, 6.0, ((0, 8), (1, 4))),
        "norm_one": jnp.clip(1.0 + 0.1 * jax.random.normal(seeds[3], (D,), jnp.float32), 0.5, 1.5).astype(jnp.bfloat16),
        "w_qkv": scatter_about(seeds[4], (D, QKV), D ** -0.5, 0.1875, ((0, 4),)),
        "b_qkv": scatter_about(seeds[5], (QKV,), 0.5, 3.0, ((0, 4),)),
        "w_out": scatter_about(seeds[6], (D, D), (D // 64) ** -0.5, 1.5, ((0, 4),)),
        "norm_two": jnp.clip(1.0 + 0.1 * jax.random.normal(seeds[7], (D,), jnp.float32), 0.5, 1.5).astype(jnp.bfloat16),
        "w_gate": scatter_about(seeds[8], (D, FF), D ** -0.5, 0.1875, ((0, 4),)),
        "w_up": scatter_about(seeds[9], (D, FF), D ** -0.5, 0.1875, ((0, 4),)),
        "w_down": scatter_about(seeds[10], (FF, D), FF ** -0.5, 0.078125, ((0, 4),)),
    }


EPSILON = 1e-06
ROPE_BASE = 1000000.0
HIGH = lax.Precision.HIGHEST

@jax.custom_vjp
def low(v):
    return lax.optimization_barrier(v.astype(jnp.bfloat16)).astype(jnp.float32)

@jax.custom_vjp
def low_back(v):
    return v

def low_keep(v):
    return (low(v), None)

def low_pass(kept, grad):
    return (grad,)

def back_keep(v):
    return (v, None)

def back_low(kept, grad):
    return (low(grad),)
low.defvjp(low_keep, low_pass)
low_back.defvjp(back_keep, back_low)

def matmul(left, right):
    return jnp.dot(left, right, precision=HIGH)

def locate(lengths, where_at):
    lengths = lengths.astype(jnp.int32)
    starts = (jnp.cumsum(lengths) - lengths).astype(jnp.int32)
    inside = where_at[:, None] >= starts[None, :]
    segment = (lax.optimization_barrier(jnp.sum(inside.astype(jnp.int32), axis=1)) - 1).astype(jnp.int32)
    opening = lax.optimization_barrier(jnp.max(jnp.where(inside, starts[None, :], 0), axis=1)).astype(jnp.int32)
    return (segment, (where_at - opening).astype(jnp.int32))

def normalize(values, gain):
    return values * lax.rsqrt(lax.optimization_barrier(jnp.mean(values * values, axis=-1, keepdims=True)) + EPSILON) * gain

def angles(places):
    half = HEAD_DIM // 2
    freqs = ROPE_BASE ** (-(jnp.arange(half, dtype=jnp.float32) * 2.0) / HEAD_DIM)
    turned = places.astype(jnp.float32)[:, None] * freqs[None, :]
    return (jnp.cos(turned)[:, None, :], jnp.sin(turned)[:, None, :])

def rotate(values, cosine, sine):
    half = values.shape[-1] // 2
    first = values[..., :half]
    second = values[..., half:]
    return jnp.concatenate([first * cosine - second * sine, second * cosine + first * sine], axis=-1)

def attend(queries, keys, values, segment):
    length = keys.shape[0]
    block = math.gcd(512, length)
    count = length // block
    index_all = jnp.arange(length, dtype=jnp.int32)
    scale = HEAD_DIM ** (-0.5)
    grouped = queries.reshape(count, block, KV_HEADS, HEADS // KV_HEADS, HEAD_DIM)

    def one_block(items):
        query_block, seg_block, index_block = items
        scores = low_back(jnp.einsum('bkgd,lkd->kgbl', query_block, keys, precision=HIGH) * scale)
        allowed = (seg_block[:, None] == segment[None, :]) & (index_all[None, :] <= index_block[:, None])
        scores = jnp.where(allowed[None, None], scores, -1e+30)
        top = lax.optimization_barrier(jnp.max(scores, axis=-1, keepdims=True))
        weights = jnp.exp(scores - top)
        probs = low(weights / lax.optimization_barrier(jnp.sum(weights, axis=-1, keepdims=True)))
        mixed = jnp.einsum('kgbl,lkd->bkgd', probs, values, precision=HIGH)
        return mixed.reshape(block, HEADS * HEAD_DIM)
    result = lax.map(jax.checkpoint(one_block), (grouped, segment.reshape(count, block), index_all.reshape(count, block)))
    return result.reshape(length, HEADS * HEAD_DIM)

def layer(inputs, norm_one, w_qkv, b_qkv, w_out, norm_two, w_gate, w_up, w_down, segment, places):
    length = inputs.shape[0]
    query_width = HEADS * HEAD_DIM
    key_width = KV_HEADS * HEAD_DIM
    hidden_one = low(normalize(inputs, norm_one))
    project = low_back(matmul(hidden_one, w_qkv) + b_qkv)
    cosine, sine = angles(places)
    queries = low(rotate(project[:, :query_width].reshape(length, HEADS, HEAD_DIM), cosine, sine))
    keys = low(rotate(project[:, query_width:query_width + key_width].reshape(length, KV_HEADS, HEAD_DIM), cosine, sine))
    values = low(project[:, query_width + key_width:].reshape(length, KV_HEADS, HEAD_DIM))
    mixed = low(low_back(attend(queries, keys, values, segment)))
    residual = inputs + low_back(matmul(mixed, w_out))
    hidden_two = low(normalize(residual, norm_two))
    gate = low_back(matmul(hidden_two, w_gate))
    upward = low_back(matmul(hidden_two, w_up))
    product = low(jax.nn.silu(gate) * upward)
    return residual + matmul(product, w_down)

def reference(tokens, doc_lengths, cotangent, norm_one, w_qkv, b_qkv, w_out, norm_two, w_gate, w_up, w_down):
    params = tuple((param.astype(jnp.float32) for param in (norm_one, w_qkv, b_qkv, w_out, norm_two, w_gate, w_up, w_down)))

    def per_sequence(totals, items):
        inputs, lengths, cotan = items
        segment, places = locate(lengths, jnp.arange(LENGTH, dtype=jnp.int32))

        def forward(inputs_f, *weights):
            return layer(inputs_f, *weights, segment, places)
        result, pull = jax.vjp(forward, inputs.astype(jnp.float32), *params)
        grads = pull(cotan.astype(jnp.float32))
        totals = tuple((total + grad for total, grad in zip(totals, grads[1:])))
        return (totals, (result.astype(jnp.bfloat16), grads[0]))
    start = tuple((jnp.zeros(param.shape, jnp.float32) for param in params))
    totals, (outputs, input_grads) = lax.scan(per_sequence, start, (tokens, doc_lengths, cotangent))
    return (outputs, input_grads, totals[0], totals[1], totals[2], totals[3], totals[4], totals[5], totals[6], totals[7])
```

```python
import functools

import jax
import jax.numpy as jnp
from jax import lax
from jax.experimental import pallas as pl
from jax.experimental.pallas import tpu as pltpu
from jax.sharding import PartitionSpec as P

HEADS = 14
KV_HEADS = 2
HEAD_DIM = 64
GROUP = HEADS // KV_HEADS
EPSILON = 1e-06
ROPE_BASE = 1000000.0
SCALE = HEAD_DIM ** (-0.5)
QB = 128
KB = 256
BF16 = jnp.bfloat16
F32 = jnp.float32


def dot_rows(left, right):
    return lax.dot_general(left, right, (((0,), (0,)), ((), ())), preferred_element_type=F32)


def dot_last(left, right):
    return lax.dot_general(left, right, (((1,), (1,)), ((), ())), preferred_element_type=F32)


def dot(left, right):
    return jnp.dot(left, right, preferred_element_type=F32)


def swap(x, axis, mask):
    return lax.ppermute(x, axis, [(i, i ^ mask) for i in range(lax.axis_size(axis))])


def after(x, *deps):
    return lax.optimization_barrier((x, *deps))[0]


def pick(x, index):
    return lax.dynamic_index_in_dim(x, index, 0, keepdims=False)


def bits_down(n):
    bits = []
    b = n // 2
    while b:
        bits.append(b)
        b //= 2
    return bits


def gather_rel(x, axis):
    blocks = {0: x}
    for b in bits_down(lax.axis_size(axis)):
        blocks.update({r ^ b: swap(v, axis, b) for r, v in list(blocks.items())})
    return blocks


def scatter_rel(parts, axis):
    parts = dict(parts)
    for b in reversed(bits_down(lax.axis_size(axis))):
        kept = {}
        for r in [r for r in parts if not r & b]:
            kept[r] = (parts[r].astype(F32) + swap(parts[r ^ b], axis, b).astype(F32)).astype(BF16)
        parts = kept
    return parts[0]


def place(blocks, index):
    rows = blocks[0].shape[0]
    out = jnp.zeros((rows * len(blocks),) + blocks[0].shape[1:], blocks[0].dtype)
    for r, v in blocks.items():
        out = lax.dynamic_update_slice_in_dim(out, v, (index ^ r) * rows, 0)
    return out


def masks(start_ref, first_query, first_key):
    key = first_key + lax.broadcasted_iota(jnp.int32, (KB, QB), 0)
    query = first_query + lax.broadcasted_iota(jnp.int32, (KB, QB), 1)
    fine = (key >= start_ref[...]) & (key <= query)
    bias = jnp.where(fine, 0.0, -1e30).astype(F32)
    return jnp.concatenate([bias] * GROUP, axis=1)


def collect(bounds, blocks, k_ref, v_ref):
    me = bounds[bounds.shape[0] - 1]
    for r, block in enumerate(blocks):
        rows = block.shape[0]
        at = pl.multiple_of((me ^ r) * rows, QB)
        k_ref[pl.ds(at, rows), :] = block[:, : 2 * HEAD_DIM]
        v_ref[pl.ds(at, rows), :] = block[:, 2 * HEAD_DIM :]


def turn_over(source, target):
    for at in range(0, source.shape[0], QB):
        target[:, at : at + QB] = source[at : at + QB, :].astype(F32).T.astype(BF16)


def forward_kernel(group, bounds, pq_ref, cos_ref, sin_ref, start_ref, *rest):
    blocks = rest[:group]
    o_ref, qt_ref, ot_ref, lse_ref, qpad, top, total, acc, k_ref, v_ref, vt_ref = rest[-11:]
    b = pl.program_id(0)

    @pl.when(b == 0)
    def _():
        collect(bounds, blocks, k_ref, v_ref)
        turn_over(v_ref, vt_ref)

    lo, hi, first = bounds[3 * b], bounds[3 * b + 1], bounds[3 * b + 2]
    half = HEAD_DIM // 2
    turned = pq_ref[...].T
    cosine, sine = cos_ref[...], sin_ref[...]
    qpad[...] = jnp.zeros_like(qpad)
    for h in range(HEADS):
        g, i = divmod(h, GROUP)
        u1 = turned[h * HEAD_DIM : h * HEAD_DIM + half]
        u2 = turned[h * HEAD_DIM + half : (h + 1) * HEAD_DIM]
        both = jnp.concatenate([u1 * cosine - u2 * sine, u2 * cosine + u1 * sine], axis=0)
        both = both.astype(BF16) * jnp.asarray(SCALE, BF16)
        qpad[g, g * HEAD_DIM : (g + 1) * HEAD_DIM, i * QB : (i + 1) * QB] = both
        qt_ref[0, g, :, i * QB : (i + 1) * QB] = both
    top[...] = jnp.full_like(top, -1e30)
    total[...] = jnp.zeros_like(total)
    acc[...] = jnp.zeros_like(acc)

    def step(j, _):
        at = pl.multiple_of(j * KB, KB)
        keys = k_ref[pl.ds(at, KB), :]
        bias = masks(start_ref, first, at)
        for g in range(KV_HEADS):
            scores = dot(keys, qpad[g]) + bias
            new_top = jnp.maximum(top[g], jnp.max(scores, axis=0, keepdims=True))
            weights = jnp.exp(scores - new_top)
            fade = jnp.exp(top[g] - new_top)
            total[g] = total[g] * fade + jnp.sum(weights, axis=0, keepdims=True)
            values = vt_ref[g * HEAD_DIM : (g + 1) * HEAD_DIM, pl.ds(at, KB)]
            acc[g] = acc[g] * fade + dot(values, weights.astype(BF16))
            top[g] = new_top
        return 0

    lax.fori_loop(lo, hi, step, 0)
    pieces = []
    for g in range(KV_HEADS):
        mixed = acc[g] / total[g]
        ot_ref[0, g] = mixed.astype(BF16)
        lse_ref[0, g] = top[g] + jnp.log(total[g])
        pieces += [mixed[:, i * QB : (i + 1) * QB] for i in range(GROUP)]
    o_ref[...] = jnp.concatenate(pieces, axis=0).T.astype(BF16)


def backward_kernel(
    group, waits, bounds, qt_ref, ot_ref, lse_ref, do_ref, cos_ref, sin_ref, start_ref, *rest
):
    blocks, rest = rest[:group], rest[group + waits :]
    dq_ref, dkv_refs, rest = rest[0], rest[1 : 1 + group], rest[1 + group :]
    qpad, dopad, qrow, dorow, centre, dqt, dk_acc, dv_acc, k_ref, v_ref, kt_ref = rest
    b = pl.program_id(0)
    lo, hi, first = bounds[3 * b], bounds[3 * b + 1], bounds[3 * b + 2]
    half = HEAD_DIM // 2

    @pl.when(b == 0)
    def _():
        dk_acc[...] = jnp.zeros_like(dk_acc)
        dv_acc[...] = jnp.zeros_like(dv_acc)
        collect(bounds, blocks, k_ref, v_ref)
        turn_over(k_ref, kt_ref)

    qpad[...] = jnp.zeros_like(qpad)
    dopad[...] = jnp.zeros_like(dopad)
    dqt[...] = jnp.zeros_like(dqt)
    grads = do_ref[...].astype(F32)
    turned = grads.T
    lane = lax.broadcasted_iota(jnp.int32, (QB, 2 * HEAD_DIM), 1)
    for h in range(HEADS):
        g, i = divmod(h, GROUP)
        rows = slice(g * HEAD_DIM, (g + 1) * HEAD_DIM)
        cols = slice(i * QB, (i + 1) * QB)
        grad_t = turned[h * HEAD_DIM : (h + 1) * HEAD_DIM]
        dopad[g, rows, cols] = grad_t.astype(BF16)
        centre[g, :, cols] = jnp.sum(grad_t * ot_ref[0, g, :, cols].astype(F32), axis=0, keepdims=True)
        query_t = qt_ref[0, g, :, cols]
        qpad[g, rows, cols] = query_t
        mine = (lane >= g * HEAD_DIM) & (lane < (g + 1) * HEAD_DIM)
        pair = grads[:, (h // 2) * 2 * HEAD_DIM : (h // 2 + 1) * 2 * HEAD_DIM]
        if h % 2 != g:
            pair = pltpu.roll(pair, HEAD_DIM, 1)
        dorow[g, cols, :] = jnp.where(mine, pair, 0.0).astype(BF16)
        wide = qpad[g, :, cols].astype(F32)
        qrow[g, cols, :] = wide.T.astype(BF16)

    def step(j, _):
        at = pl.multiple_of(j * KB, KB)
        keys = k_ref[pl.ds(at, KB), :]
        values = v_ref[pl.ds(at, KB), :]
        bias = masks(start_ref, first, at)
        dk_term = None
        dv_term = None
        for g in range(KV_HEADS):
            probs = jnp.exp(dot(keys, qpad[g]) + bias - lse_ref[0, g])
            grad_probs = dot(values, dopad[g])
            grad_scores = (probs * (grad_probs - centre[g])).astype(BF16)
            dv_g = dot(probs.astype(BF16), dorow[g])
            dk_g = dot(grad_scores, qrow[g])
            dk_term = dk_g if g == 0 else dk_term + dk_g
            dv_term = dv_g if g == 0 else dv_term + dv_g
            turned_keys = kt_ref[g * HEAD_DIM : (g + 1) * HEAD_DIM, pl.ds(at, KB)]
            dqt[g] += dot(turned_keys, grad_scores)
        dk_acc[pl.ds(at, KB), :] += dk_term
        dv_acc[pl.ds(at, KB), :] += dv_term
        return 0

    lax.fori_loop(lo, hi, step, 0)
    cosine, sine = cos_ref[...], sin_ref[...]
    pieces = []
    for h in range(HEADS):
        g, i = divmod(h, GROUP)
        w1 = dqt[g, :half, i * QB : (i + 1) * QB] * SCALE
        w2 = dqt[g, half:, i * QB : (i + 1) * QB] * SCALE
        pieces += [w1 * cosine + w2 * sine, w2 * cosine - w1 * sine]
    dq_ref[...] = jnp.concatenate(pieces, axis=0).T.astype(BF16)

    @pl.when(b == pl.num_programs(0) - 1)
    def _():
        me = bounds[bounds.shape[0] - 1]
        for r, ref in enumerate(dkv_refs):
            rows = ref.shape[0]
            at = pl.multiple_of((me ^ r) * rows, QB)
            ref[:, : 2 * HEAD_DIM] = dk_acc[pl.ds(at, rows), :].astype(BF16)
            ref[:, 2 * HEAD_DIM :] = dv_acc[pl.ds(at, rows), :].astype(BF16)


def whole(shape):
    return pl.BlockSpec(shape, lambda b, *_: (0,) * len(shape))


def attention_forward(bounds, pq, cos_t, sin_t, start, blocks, waits):
    rows = pq.shape[0]
    length = rows * len(blocks)
    count = rows // QB
    width = HEADS * HEAD_DIM
    lanes = GROUP * QB
    return pl.pallas_call(
        functools.partial(forward_kernel, len(blocks)),
        out_shape=(
            jax.ShapeDtypeStruct((rows, width), BF16),
            jax.ShapeDtypeStruct((count, KV_HEADS, HEAD_DIM, lanes), BF16),
            jax.ShapeDtypeStruct((count, KV_HEADS, HEAD_DIM, lanes), BF16),
            jax.ShapeDtypeStruct((count, KV_HEADS, 1, lanes), F32),
        ),
        grid_spec=pltpu.PrefetchScalarGridSpec(
            num_scalar_prefetch=1,
            grid=(count,),
            in_specs=[
                pl.BlockSpec((QB, width), lambda b, *_: (b, 0)),
                pl.BlockSpec((HEAD_DIM // 2, QB), lambda b, *_: (0, b)),
                pl.BlockSpec((HEAD_DIM // 2, QB), lambda b, *_: (0, b)),
                pl.BlockSpec((1, QB), lambda b, *_: (0, b)),
                *[whole((rows, 4 * HEAD_DIM))] * len(blocks),
                *[pl.BlockSpec(memory_space=pl.ANY)] * len(waits),
            ],
            out_specs=[
                pl.BlockSpec((QB, width), lambda b, *_: (b, 0)),
                pl.BlockSpec((1, KV_HEADS, HEAD_DIM, lanes), lambda b, *_: (b, 0, 0, 0)),
                pl.BlockSpec((1, KV_HEADS, HEAD_DIM, lanes), lambda b, *_: (b, 0, 0, 0)),
                pl.BlockSpec((1, KV_HEADS, 1, lanes), lambda b, *_: (b, 0, 0, 0)),
            ],
            scratch_shapes=[
                pltpu.VMEM((KV_HEADS, 2 * HEAD_DIM, lanes), BF16),
                pltpu.VMEM((KV_HEADS, 1, lanes), F32),
                pltpu.VMEM((KV_HEADS, 1, lanes), F32),
                pltpu.VMEM((KV_HEADS, HEAD_DIM, lanes), F32),
                pltpu.VMEM((length, 2 * HEAD_DIM), BF16),
                pltpu.VMEM((length, 2 * HEAD_DIM), BF16),
                pltpu.VMEM((2 * HEAD_DIM, length), BF16),
            ],
        ),
        compiler_params=pltpu.CompilerParams(vmem_limit_bytes=40 << 20),
        cost_estimate=pl.CostEstimate(
            flops=1 << 22, bytes_accessed=1 << 18, transcendentals=0
        ),
        name="attention_forward",
    )(bounds, pq, cos_t, sin_t, start, *blocks, *waits)


def attention_backward(bounds, qt, ot, lse, grad_mixed, cos_t, sin_t, start, blocks, waits):
    rows = grad_mixed.shape[0]
    group = len(blocks)
    length = rows * group
    count = rows // QB
    width = HEADS * HEAD_DIM
    lanes = GROUP * QB
    return pl.pallas_call(
        functools.partial(backward_kernel, group, len(waits)),
        out_shape=(
            jax.ShapeDtypeStruct((rows, width), BF16),
            *[jax.ShapeDtypeStruct((rows, 4 * HEAD_DIM), BF16)] * group,
        ),
        grid_spec=pltpu.PrefetchScalarGridSpec(
            num_scalar_prefetch=1,
            grid=(count,),
            in_specs=[
                pl.BlockSpec((1, KV_HEADS, HEAD_DIM, lanes), lambda b, *_: (b, 0, 0, 0)),
                pl.BlockSpec((1, KV_HEADS, HEAD_DIM, lanes), lambda b, *_: (b, 0, 0, 0)),
                pl.BlockSpec((1, KV_HEADS, 1, lanes), lambda b, *_: (b, 0, 0, 0)),
                pl.BlockSpec((QB, width), lambda b, *_: (b, 0)),
                pl.BlockSpec((HEAD_DIM // 2, QB), lambda b, *_: (0, b)),
                pl.BlockSpec((HEAD_DIM // 2, QB), lambda b, *_: (0, b)),
                pl.BlockSpec((1, QB), lambda b, *_: (0, b)),
                *[whole((rows, 4 * HEAD_DIM))] * group,
                *[pl.BlockSpec(memory_space=pl.ANY)] * len(waits),
            ],
            out_specs=[
                pl.BlockSpec((QB, width), lambda b, *_: (b, 0)),
                *[whole((rows, 4 * HEAD_DIM))] * group,
            ],
            scratch_shapes=[
                pltpu.VMEM((KV_HEADS, 2 * HEAD_DIM, lanes), BF16),
                pltpu.VMEM((KV_HEADS, 2 * HEAD_DIM, lanes), BF16),
                pltpu.VMEM((KV_HEADS, lanes, 2 * HEAD_DIM), BF16),
                pltpu.VMEM((KV_HEADS, lanes, 2 * HEAD_DIM), BF16),
                pltpu.VMEM((KV_HEADS, 1, lanes), F32),
                pltpu.VMEM((KV_HEADS, HEAD_DIM, lanes), F32),
                pltpu.VMEM((length, 2 * HEAD_DIM), F32),
                pltpu.VMEM((length, 2 * HEAD_DIM), F32),
                pltpu.VMEM((length, 2 * HEAD_DIM), BF16),
                pltpu.VMEM((length, 2 * HEAD_DIM), BF16),
                pltpu.VMEM((2 * HEAD_DIM, length), BF16),
            ],
        ),
        compiler_params=pltpu.CompilerParams(vmem_limit_bytes=48 << 20),
        cost_estimate=pl.CostEstimate(
            flops=1 << 22, bytes_accessed=1 << 18, transcendentals=0
        ),
        name="attention_backward",
    )(bounds, qt, ot, lse, grad_mixed, cos_t, sin_t, start, *blocks, *waits)


def project_kernel(offsets, x_ref, gain_ref, bias_ref, cos_ref, sin_ref, *rest):
    pieces = rest[:-6]
    pass_ref, q_ref, kv_ref, hidden_ref, w_ref, passed_ref = rest[-6:]
    passed_ref[...] = pass_ref[...]
    for i, piece in enumerate(pieces):
        count = piece.shape[0]
        w_ref[pl.ds(pl.multiple_of(offsets[i], 16), count), :] = piece[...]
    x = x_ref[...].astype(F32)
    scale = lax.rsqrt(jnp.mean(x * x, axis=-1, keepdims=True) + EPSILON)
    hidden = (x * scale * gain_ref[...]).astype(BF16)
    hidden_ref[...] = hidden
    query_width = HEADS * HEAD_DIM
    key_width = KV_HEADS * HEAD_DIM
    q_ref[...] = dot(hidden, w_ref[:, :query_width]) + bias_ref[:, :query_width]
    kv = dot(hidden, w_ref[:, query_width:]) + bias_ref[:, query_width:]
    keys = kv[:, :key_width]
    lane = lax.broadcasted_iota(jnp.int32, keys.shape, 1) % HEAD_DIM
    half = HEAD_DIM // 2
    other = jnp.where(
        lane < half, pltpu.roll(keys, key_width - half, 1), pltpu.roll(keys, half, 1)
    )
    keys = keys * cos_ref[...] + other * sin_ref[...]
    kv_ref[:, :key_width] = keys.astype(BF16)
    kv_ref[:, key_width:] = kv[:, key_width:].astype(BF16)


def project(offsets, x, gain, bias, cosine, sine, pieces, passed):
    rows, width = x.shape
    total = bias.shape[1]
    query_width = HEADS * HEAD_DIM
    return pl.pallas_call(
        project_kernel,
        out_shape=(
            jax.ShapeDtypeStruct((rows, query_width), F32),
            jax.ShapeDtypeStruct((rows, total - query_width), BF16),
            jax.ShapeDtypeStruct((rows, width), BF16),
            jax.ShapeDtypeStruct((width, total), BF16),
            jax.ShapeDtypeStruct(passed.shape, BF16),
        ),
        grid_spec=pltpu.PrefetchScalarGridSpec(
            num_scalar_prefetch=1,
            grid=(1,),
            in_specs=[whole(v.shape) for v in (x, gain, bias, cosine, sine, *pieces, passed)],
            out_specs=[
                whole((rows, query_width)),
                whole((rows, total - query_width)),
                whole((rows, width)),
                whole((width, total)),
                whole(passed.shape),
            ],
        ),
        compiler_params=pltpu.CompilerParams(vmem_limit_bytes=40 << 20),
        cost_estimate=pl.CostEstimate(
            flops=2 * rows * width * total, bytes_accessed=8 << 20, transcendentals=0
        ),
        name="norm_project_rotate",
    )(offsets, x, gain, bias, cosine, sine, *pieces, passed)


def output_kernel(pieces, offsets, x_ref, mixed_ref, gain_ref, *rest):
    residual_ref, hidden_ref, w_ref = rest[-3:]
    for i, piece in enumerate(rest[:pieces]):
        w_ref[pl.ds(pl.multiple_of(offsets[i], 16), piece.shape[0]), :] = piece[...]
    residual = x_ref[...].astype(F32) + dot(mixed_ref[...], w_ref[...])
    residual_ref[...] = residual
    scale = lax.rsqrt(jnp.mean(residual * residual, axis=-1, keepdims=True) + EPSILON)
    hidden_ref[...] = (residual * scale * gain_ref[...]).astype(BF16)


def output_of(offsets, x, mixed, gain, pieces, waits):
    rows, width = x.shape
    return pl.pallas_call(
        functools.partial(output_kernel, len(pieces)),
        out_shape=(
            jax.ShapeDtypeStruct((rows, width), F32),
            jax.ShapeDtypeStruct((rows, width), BF16),
            jax.ShapeDtypeStruct((width, width), BF16),
        ),
        grid_spec=pltpu.PrefetchScalarGridSpec(
            num_scalar_prefetch=1,
            grid=(1,),
            in_specs=[
                *[whole(v.shape) for v in (x, mixed, gain, *pieces)],
                *[pl.BlockSpec(memory_space=pl.ANY)] * len(waits),
            ],
            out_specs=[whole((rows, width)), whole((rows, width)), whole((width, width))],
        ),
        compiler_params=pltpu.CompilerParams(vmem_limit_bytes=40 << 20),
        cost_estimate=pl.CostEstimate(flops=1 << 22, bytes_accessed=1 << 18, transcendentals=0),
        name="project_add_norm",
    )(offsets, x, mixed, gain, *pieces, *waits)


FB = 256


def feed_kernel(blocks, offsets, *refs):
    hs, dys, refs = refs[:blocks], refs[blocks : 2 * blocks], refs[2 * blocks :]
    count = offsets.shape[0]
    pieces, refs = refs[:count], refs[count:]
    wd_ref, m_ref, d_ref = refs[:3]
    outs, backs = refs[3 : 3 + blocks], refs[3 + blocks : 3 + 2 * blocks]
    out_acc, dh_acc, wg, wu = refs[3 + 2 * blocks :]
    step = pl.program_id(0)
    last = pl.num_programs(0) - 1
    rows = hs[0].shape[0]
    for i, piece in enumerate(pieces):
        at = pl.ds(pl.multiple_of(offsets[i], 16), piece.shape[1])
        wg[at, :] = piece[0]
        wu[at, :] = piece[1]

    @pl.when(step == 0)
    def _():
        out_acc[...] = jnp.zeros_like(out_acc)
        dh_acc[...] = jnp.zeros_like(dh_acc)

    for t in range(blocks):
        at = slice(t * rows, (t + 1) * rows)
        hidden, cot = hs[t][...], dys[t][...]
        gate = dot(hidden, wg[...])
        upward = dot(hidden, wu[...])
        grad_product = dot_last(cot, wd_ref[...])
        sigma = jax.nn.sigmoid(gate)
        active = gate * sigma
        product = (active * upward).astype(BF16)
        grad_gate = (grad_product * upward * (sigma + active * (1.0 - sigma))).astype(BF16)
        grad_up = (grad_product * active).astype(BF16)
        d_ref[0, at], d_ref[1, at] = grad_gate, grad_up
        m_ref[:, at] = (active * upward).T.astype(BF16)
        out_acc[at] += dot(product, wd_ref[...])
        dh_acc[at] += dot_last(grad_gate, wg[...]) + dot_last(grad_up, wu[...])

    @pl.when(step == last)
    def _():
        for t in range(blocks):
            at = slice(t * rows, (t + 1) * rows)
            outs[t][...] = out_acc[at].astype(BF16)
            backs[t][...] = dh_acc[at].astype(BF16)


def feed(offsets, hiddens, cots, pieces, w_down):
    blocks = len(hiddens)
    rows, width = hiddens[0].shape
    inner = w_down.shape[0]
    wide = jax.ShapeDtypeStruct((2, blocks * rows, inner), BF16)
    tall = jax.ShapeDtypeStruct((inner, blocks * rows), BF16)
    narrow = jax.ShapeDtypeStruct((rows, width), BF16)
    return pl.pallas_call(
        functools.partial(feed_kernel, blocks),
        out_shape=(tall, wide) + (narrow,) * (2 * blocks),
        grid_spec=pltpu.PrefetchScalarGridSpec(
            num_scalar_prefetch=1,
            grid=(inner // FB,),
            in_specs=[
                *[whole((rows, width))] * (2 * blocks),
                *[pl.BlockSpec((2, v.shape[1], FB), lambda j, *_: (0, 0, j)) for v in pieces],
                pl.BlockSpec((FB, width), lambda j, *_: (j, 0)),
            ],
            out_specs=[
                pl.BlockSpec((FB, blocks * rows), lambda j, *_: (j, 0)),
                pl.BlockSpec((2, blocks * rows, FB), lambda j, *_: (0, 0, j)),
                *[whole((rows, width))] * (2 * blocks),
            ],
            scratch_shapes=[
                pltpu.VMEM((blocks * rows, width), F32),
                pltpu.VMEM((blocks * rows, width), F32),
                pltpu.VMEM((width, FB), BF16),
                pltpu.VMEM((width, FB), BF16),
            ],
        ),
        compiler_params=pltpu.CompilerParams(vmem_limit_bytes=48 << 20),
        cost_estimate=pl.CostEstimate(
            flops=1 << 22, bytes_accessed=1 << 18, transcendentals=0
        ),
        name="feed_forward_backward",
    )(offsets, *hiddens, *cots, *pieces, w_down)


def down_kernel(parts, per, cut, offsets, *refs):
    ms, dys, outs = refs[:parts], refs[parts : parts + parts * per], refs[-2:]
    for k, out_ref in enumerate(outs):
        rows = out_ref.shape[0]

        @pl.when(pl.program_id(0) == 1 - k)
        def _():
            total = None
            for i, m_ref in enumerate(ms):
                width = m_ref.shape[-1] // per
                for t in range(per):
                    if cut:
                        at = pl.ds(pl.multiple_of(offsets[k], 16), rows)
                        left = m_ref[at, t * width : (t + 1) * width]
                    else:
                        left = m_ref[k, :, t * width : (t + 1) * width]
                    term = dot(left, dys[i * per + t][...])
                    total = term if total is None else total + term
            out_ref[...] = total.astype(BF16)


def grad_down_of(products, cots, offsets, half, waits):
    rows, width = cots[0].shape
    cut = half % 16 == 0
    if not cut:
        products = [
            jnp.stack([lax.dynamic_slice_in_dim(v, offsets[k], half, 0) for k in range(2)]) for v in products
        ]
    out = jax.ShapeDtypeStruct((half, width), BF16)
    return pl.pallas_call(
        functools.partial(down_kernel, len(products), len(cots) // len(products), cut),
        out_shape=(out, out),
        grid_spec=pltpu.PrefetchScalarGridSpec(
            num_scalar_prefetch=1,
            grid=(2,),
            in_specs=[*[whole(v.shape) for v in (*products, *cots)], *[ANY] * len(waits)],
            out_specs=[whole((half, width))] * 2,
        ),
        compiler_params=pltpu.CompilerParams(vmem_limit_bytes=56 << 20),
        cost_estimate=pl.CostEstimate(flops=1 << 22, bytes_accessed=1 << 18, transcendentals=0),
        name="grad_down",
    )(offsets, *products, *cots, *waits)


def gate_up_kernel(parts, blocks, waits, given, which, *refs):
    keeps, sends, refs = refs[:parts], refs[parts : 2 * parts], refs[2 * parts :]
    hs, refs = refs[:blocks], refs[blocks + waits :]
    outs, refs = refs[:2], refs[2:]
    if given:
        (turned,) = hs
    else:
        (turned,) = refs

        @pl.when(pl.program_id(0) == 0)
        def _():
            rows = hs[0].shape[0]
            for t, h in enumerate(hs):
                for at in range(0, rows, QB):
                    place_at = slice(t * rows + at, t * rows + at + QB)
                    turned[:, place_at] = h[at : at + QB, :].astype(F32).T.astype(BF16)

    for out, group in zip(outs, (keeps, sends)):
        total = None
        first = 0
        for v in group:
            term = dot(turned[:, first : first + v.shape[1]], v[0])
            total = term if total is None else total + term
            first += v.shape[1]
        out[...] = total.astype(BF16)


def grad_gate_up_of(grads, hiddens, first, count, which, waits):
    given = len(hiddens) == 1
    width = hiddens[0].shape[0] if given else hiddens[0].shape[1]
    tokens = sum(v.shape[1] for v in grads)
    out = jax.ShapeDtypeStruct((width, count * FB), BF16)
    turned = jax.ShapeDtypeStruct((width, tokens), BF16)
    place_of = pl.BlockSpec((width, FB), lambda j, *_: (0, j))
    keep = [pl.BlockSpec((1, v.shape[1], FB), lambda j, at: (at[0], 0, j + first)) for v in grads]
    send = [pl.BlockSpec((1, v.shape[1], FB), lambda j, at: (1 - at[0], 0, j + first)) for v in grads]
    return pl.pallas_call(
        functools.partial(gate_up_kernel, len(grads), len(hiddens), len(waits), given),
        out_shape=(out, out) if given else (out, out, turned),
        grid_spec=pltpu.PrefetchScalarGridSpec(
            num_scalar_prefetch=1,
            grid=(count,),
            in_specs=[*keep, *send, *[whole(v.shape) for v in hiddens], *[ANY] * len(waits)],
            out_specs=[place_of] * 2 if given else [place_of] * 2 + [whole((width, tokens))],
        ),
        compiler_params=pltpu.CompilerParams(vmem_limit_bytes=56 << 20),
        cost_estimate=pl.CostEstimate(flops=1 << 22, bytes_accessed=1 << 18, transcendentals=0),
        name="grad_gate_up",
    )(which, *grads, *grads, *hiddens, *waits)


def residual_back_kernel(mine_ref, got_ref, cot_ref, residual_ref, gain_ref, w_ref, *rest):
    grad_ref, mixed_ref, gain_out = rest[-3:]
    grad_hidden = mine_ref[...].astype(F32) + got_ref[...].astype(F32)
    residual = residual_ref[...]
    scale = lax.rsqrt(jnp.mean(residual * residual, axis=-1, keepdims=True) + EPSILON)
    normed = residual * scale
    gain_out[...] = jnp.sum(grad_hidden * normed, axis=0, keepdims=True)
    grad = cot_ref[...].astype(F32) + norm_back(grad_hidden, normed, scale, gain_ref[...])
    grad_ref[...] = grad
    mixed_ref[...] = dot_last(grad.astype(BF16), w_ref[...]).astype(BF16)


def single_call(kernel, name, ins, waits, outs, scalars=None):
    scalars = jnp.zeros((1,), jnp.int32) if scalars is None else scalars
    scratch = [v for v in outs if isinstance(v, type(pltpu.VMEM((8, 128), F32)))]
    outs = [v for v in outs if v not in scratch]

    def body(scalar_ref, *refs):
        kernel(scalar_ref, *refs[: len(ins)], *refs[len(ins) + len(waits) :])

    return pl.pallas_call(
        body,
        out_shape=outs,
        grid_spec=pltpu.PrefetchScalarGridSpec(
            num_scalar_prefetch=1,
            grid=(1,),
            in_specs=[*[whole(v.shape) for v in ins], *[ANY] * len(waits)],
            out_specs=[whole(v.shape) for v in outs],
            scratch_shapes=scratch,
        ),
        compiler_params=pltpu.CompilerParams(vmem_limit_bytes=52 << 20),
        cost_estimate=pl.CostEstimate(flops=1 << 22, bytes_accessed=1 << 18, transcendentals=0),
        name=name,
    )(scalars, *ins, *waits)


def project_back_kernel(
    aligned, offsets, x_ref, gain_ref, hidden_ref, dq_ref, mine_ref, got_ref, w_ref, grad_ref, mixed_ref,
    cos_ref, sin_ref, out_ref, gain_out, bias_out, *rest
):
    weights, (dp_ref, dw_ref) = rest[:-2], rest[-2:]
    query_width = HEADS * HEAD_DIM
    key_width = KV_HEADS * HEAD_DIM
    half = HEAD_DIM // 2
    total = w_ref.shape[1]
    dkv = mine_ref[...].astype(F32) + got_ref[...].astype(F32)
    keys = dkv[:, :key_width]
    lane = lax.broadcasted_iota(jnp.int32, keys.shape, 1) % HEAD_DIM
    other = jnp.where(
        lane < half, pltpu.roll(keys, key_width - half, 1), pltpu.roll(keys, half, 1)
    )
    dp_ref[:, :query_width] = dq_ref[...]
    dp_ref[:, query_width : query_width + key_width] = (
        keys * cos_ref[...] - other * sin_ref[...]
    ).astype(BF16)
    dp_ref[:, query_width + key_width :] = dkv[:, key_width:].astype(BF16)
    grads = dp_ref[...]
    bias_out[...] = jnp.sum(grads.astype(F32), axis=0, keepdims=True)
    back = dot_last(grads, w_ref[...])
    x = x_ref[...].astype(F32)
    scale = lax.rsqrt(jnp.mean(x * x, axis=-1, keepdims=True) + EPSILON)
    normed = x * scale
    gain_out[...] = jnp.sum(back * normed, axis=0, keepdims=True)
    out_ref[...] = grad_ref[...] + norm_back(back, normed, scale, gain_ref[...])
    dw_ref[:, :total] = dot(hidden_ref[...].astype(F32).T.astype(BF16), grads).astype(BF16)
    dw_ref[:, total:] = dot(
        mixed_ref[...].astype(F32).T.astype(BF16), grad_ref[...].astype(BF16)
    ).astype(BF16)
    if aligned:
        rows = dw_ref.shape[0] // len(weights)
        for k, ref in enumerate(weights):
            ref[:rows] = dw_ref[pl.ds(pl.multiple_of(offsets[k], 16), rows), :]
            ref[rows:] = jnp.zeros((ref.shape[0] - rows, ref.shape[1]), BF16)
    else:
        weights[0][...] = dw_ref[...]


ANY = pl.BlockSpec(memory_space=pl.ANY)


class Line:
    def __init__(self):
        self.last = []

    def mark(self, x):
        self.last = [x]
        return x


def small_call(kernel, name, scalars, grid, ins, in_specs, out_shape, out_specs, waits):
    count = len(ins)

    def body(scalar_ref, *refs):
        kernel(scalar_ref, refs[:count], refs[count + len(waits) :])

    return pl.pallas_call(
        body,
        out_shape=out_shape,
        grid_spec=pltpu.PrefetchScalarGridSpec(
            num_scalar_prefetch=1,
            grid=grid,
            in_specs=[*in_specs, *[ANY] * len(waits)],
            out_specs=out_specs,
        ),
        compiler_params=pltpu.CompilerParams(vmem_limit_bytes=40 << 20),
        cost_estimate=pl.CostEstimate(flops=1 << 20, bytes_accessed=1 << 18, transcendentals=0),
        name=name,
    )(scalars, *ins, *waits)


def add_split(x, got, lead, mine, waits):
    columns = x.shape[-1]
    x, got = x.reshape(lead, 2, -1, columns), got.reshape(lead, 2, -1, columns)
    rows = x.shape[2]

    def kernel(_, ins, outs):
        for k in range(2):
            total = ins[2 * k][0, 0].astype(F32) + ins[2 * k + 1][0, 0].astype(F32)
            outs[k][0] = total.astype(BF16)

    keep = pl.BlockSpec((1, 1, rows, columns), lambda i, at: (i, at[0], 0, 0))
    send = pl.BlockSpec((1, 1, rows, columns), lambda i, at: (i, 1 - at[0], 0, 0))
    half = jax.ShapeDtypeStruct((lead, rows, columns), BF16)
    out = pl.BlockSpec((1, rows, columns), lambda i, at: (i, 0, 0))
    return small_call(
        kernel, "add_and_split", mine[None], (lead,), (x, got, x, got), (keep, keep, send, send),
        (half, half), (out, out), waits,
    )


def add_ordered(x, got, order, waits):
    shape = (1,) + x.shape[1:]
    got = got.reshape(x.shape)

    def kernel(_, ins, outs):
        for k, out in enumerate(outs):
            out[...] = (ins[2 * k][...].astype(F32) + ins[2 * k + 1][...].astype(F32)).astype(BF16)

    specs = []
    for k in range(order.shape[0]):
        specs += [pl.BlockSpec(shape, lambda i, at, k=k: (at[k], 0, 0))] * 2
    count = order.shape[0]
    return small_call(
        kernel, "add", order, (1,), (x, got) * count, specs,
        (jax.ShapeDtypeStruct(shape, BF16),) * count, (whole(shape),) * count, waits,
    )


def put_ordered(parts, order, waits, dtype=BF16):
    shape = parts[0].shape
    block = shape[-2:]
    lead = parts[0].size // (block[0] * block[1])
    parts = [v.reshape((lead,) + block) for v in parts]
    count = len(parts)

    def kernel(at, ins, outs):
        for k in range(count):
            outs[0][at[k]] = ins[k][...].astype(dtype)

    (out,) = small_call(
        kernel, "place", order, (lead,), parts,
        [pl.BlockSpec((1,) + block, lambda i, at: (i, 0, 0))] * count,
        (jax.ShapeDtypeStruct((count, lead) + block, dtype),),
        (pl.BlockSpec((count, 1) + block, lambda i, at: (0, i, 0, 0)),), waits,
    )
    return out.reshape((count,) + shape)


def steps_of_sum(line, keep, send, lead, order=None, last=None, bits=None):
    index = lax.axis_index("dp")
    depth = lax.axis_size("dp").bit_length() - 1
    masks = [1 << k for k in (range(depth) if bits is None else bits)]
    bits = [((index // mask) & 1).astype(jnp.int32) for mask in masks]
    pair = lambda k: jnp.stack([bits[k], 1 - bits[k]])
    columns = keep.shape[-1]
    for k in range(depth - 1):
        got = swap(send, "dp", masks[k])
        yield None
        keep, send = add_split(keep, got, lead, bits[k + 1], line.last)
        line.mark(keep)
    got = swap(send, "dp", masks[-1])
    yield None
    keep = keep.reshape(lead, -1, columns)
    if order is None:
        (part,) = add_ordered(keep, got, jnp.zeros((1,), jnp.int32), line.last)
        part = line.mark(part[0])
    else:
        parts = add_ordered(keep, got, order, line.last)
        line.mark(parts[0])
        parts = [swap(v, "seq", r) if r else v for r, v in enumerate(parts)]
        yield None
        part = line.mark(put_ordered([v[0] for v in parts], order, line.last))
    for k in reversed(range(1, depth)):
        got = swap(part, "dp", masks[k])
        yield None
        part = line.mark(put_ordered([part, got], pair(k), line.last))
    got = swap(part, "dp", masks[0])
    yield None
    part = put_ordered([part, got], pair(0), line.last, BF16 if last is None else last)
    line.mark(part)
    yield part


def steps_of_scatter(parts, axis):
    parts = dict(parts)
    for b in reversed(bits_down(lax.axis_size(axis))):
        got = {r: swap(parts[r ^ b], axis, b) for r in parts if not r & b}
        yield None
        if len(got) == 1:
            yield parts[0], got[0]
        parts = {r: (parts[r].astype(F32) + v.astype(F32)).astype(BF16) for r, v in got.items()}


def pad_rows(x, multiple):
    extra = -x.shape[0] % multiple
    return jnp.pad(x, ((0, extra), (0, 0))) if extra else x


def locate(lengths, where_at):
    starts = jnp.cumsum(lengths) - lengths
    inside = where_at[:, None] >= starts[None, :]
    return jnp.max(jnp.where(inside, starts[None, :], 0), axis=1)


def norm_back(grad_hidden, normed, scale_rows, gain):
    scaled = grad_hidden * gain
    return scale_rows * (scaled - normed * jnp.mean(scaled * normed, axis=-1, keepdims=True))


def turn_heads(values, cosine, sine):
    rows = values.shape[0]
    values = values.reshape(rows, KV_HEADS, HEAD_DIM)
    half = HEAD_DIM // 2
    first, second = values[..., :half], values[..., half:]
    cosine, sine = cosine[:, None, :], sine[:, None, :]
    turned = jnp.concatenate([first * cosine - second * sine, second * cosine + first * sine], axis=-1)
    return turned.reshape(rows, KV_HEADS * HEAD_DIM)


def swaps(x, axis):
    return {r: swap(x, axis, r) if r else x for r in range(lax.axis_size(axis))}


def windows(total, count, tile=128):
    each = total // count
    firsts = [j * each // tile * tile for j in range(count)]
    width = max(j * each - first + each for j, first in enumerate(firsts))
    return -(-width // FB) * FB, firsts


def join(parts, firsts, total, tile=128):
    runs = []
    for at in range(0, total, tile):
        cover = []
        for i, (first, values) in enumerate(parts):
            for j, begin in enumerate(firsts):
                local = at - begin - first
                if 0 <= local < values.shape[-1]:
                    cover.append((i, j, local))
        if runs and [(i, j, c - runs[-1][1]) for i, j, c in cover] == runs[-1][0]:
            runs[-1][1] += tile
        else:
            runs.append([cover, tile])
    segments = []
    for cover, width in runs:
        segments.append(
            sum(parts[i][1][j, :, c : c + width].astype(F32) for i, j, c in cover)
        )
    return jnp.concatenate(segments, axis=1)


def per_device(
    tokens, doc_lengths, cotangent, norm_one, w_qkv, b_qkv, w_out, norm_two, w_gate, w_up, w_down
):
    group = lax.axis_size("seq")
    me = lax.axis_index("seq")
    inputs = tokens[0].astype(F32)
    rows, width = inputs.shape
    query_width = HEADS * HEAD_DIM
    key_width = KV_HEADS * HEAD_DIM
    slice_d = width // group
    slice_b = b_qkv.shape[0]
    slice_f = w_down.shape[0]
    hidden_units = slice_f * group
    aligned = slice_d % 32 == 0

    small = jnp.concatenate([norm_one, norm_two, b_qkv])[None, :]
    small = place(swaps(small, "seq"), me)
    gain_one = small[:, :slice_d].reshape(1, width).astype(F32)
    gain_two = small[:, slice_d : 2 * slice_d].reshape(1, width).astype(F32)
    bias = small[:, 2 * slice_d :].reshape(1, -1).astype(F32)
    pieces_qkv = gather_rel(w_qkv, "seq")
    order = [me ^ r for r in range(group)]
    if aligned:
        offsets_qkv = jnp.stack([j * slice_d for j in order]).astype(jnp.int32)
        pieces_qkv = [pieces_qkv[r] for r in range(group)]
    else:
        offsets_qkv = jnp.zeros((1,), jnp.int32)
        pieces_qkv = [place(pieces_qkv, me)]

    inner, firsts = windows(hidden_units, group)
    both = jnp.stack([w_gate, w_up])
    both = jnp.pad(both, ((0, 0), (0, 0), (0, max(0, firsts[-1] + inner - hidden_units))))
    both = jnp.stack([both[:, :, at : at + inner] for at in firsts])
    shift = lax.rem(me * slice_f, 128)
    down = lax.dynamic_update_slice_in_dim(jnp.zeros((inner, width), BF16), w_down, shift, 0)

    half_d = slice_d // 2
    fast = (lax.axis_index("dp") & 1).astype(jnp.int32)
    slow = ((lax.axis_index("dp") >> 1) & 1).astype(jnp.int32)
    early = {}
    for r in range(2, group):
        part = lax.dynamic_slice(
            both, (order[r], slow, fast * half_d, 0), (1, 1, half_d, inner)
        )
        early[r] = swap(part.reshape(half_d, inner), "seq", r)

    offset = me * rows
    index = offset + jnp.arange(rows, dtype=jnp.int32)
    start = locate(doc_lengths[0], index)
    places = (index - start).astype(F32)
    half = HEAD_DIM // 2
    freqs = ROPE_BASE ** (-(jnp.arange(half, dtype=F32) * 2.0) / HEAD_DIM)
    angle = places[:, None] * freqs[None, :]
    cosine, sine = jnp.cos(angle), jnp.sin(angle)
    cos_t, sin_t = cosine.T, sine.T
    cos_k = jnp.concatenate([cosine] * (2 * KV_HEADS), axis=1)
    sin_k = jnp.concatenate([-sine, sine] * KV_HEADS, axis=1)
    marks = offset + jnp.arange(rows // QB, dtype=jnp.int32) * QB
    bounds = jnp.stack([start[::QB] // KB, (marks + QB - 1) // KB + 1, marks], axis=1).reshape(-1)
    bounds = jnp.concatenate([bounds, me[None]]).astype(jnp.int32)
    start_row = start.astype(jnp.int32)[None, :]

    queries, kv, hidden_one, full_qkv, w_out = project(
        offsets_qkv, tokens[0], gain_one, bias, cos_k, sin_k, pieces_qkv, w_out
    )
    pieces_out = gather_rel(w_out, "seq")
    pieces_out = [pieces_out[r] for r in range(group)] if aligned else [place(pieces_out, me)]
    (kv,) = single_call(
        lambda _, a, b: b.__setitem__(..., a[...]), "pass_on", (kv,), [early[r] for r in early],
        [jax.ShapeDtypeStruct(kv.shape, BF16)],
    )
    blocks = gather_rel(kv, "seq")
    blocks = [blocks[r] for r in range(group)]
    later = {}
    pieces = [pick(both, order[0]), swap(pick(both, order[1]), "seq", 1)]
    offsets = [order[0] * slice_d, order[1] * slice_d]
    for r in range(2, group):
        later[r] = got = swap(early[r], "dp", 2)
        part = jnp.stack([jnp.where(slow == 0, early[r], got), jnp.where(slow == 0, got, early[r])])
        pieces += [part, swap(part, "dp", 1)]
        at = order[r] * slice_d
        offsets += [at + fast * half_d, at + (1 - fast) * half_d]
    if not aligned:
        full = jnp.zeros((2, width, inner), BF16)
        for piece, at in zip(pieces, offsets):
            full = lax.dynamic_update_slice(full, piece, (0, at, 0))
        pieces, offsets = [full], [0 * me]
    offsets = jnp.stack(offsets).astype(jnp.int32)
    mixed, qt, ot, lse = attention_forward(bounds, queries, cos_t, sin_t, start_row, blocks, [])
    residual, hidden_two, full_out = output_of(
        offsets_qkv, tokens[0], mixed, gain_two, pieces_out, [later[r] for r in later]
    )

    cot = cotangent[0]
    hiddens = gather_rel(hidden_two, "seq")
    cots = gather_rel(after(cot, hiddens[group // 2]), "seq")
    terms_out, terms_back, products, grads = {}, {}, [], []
    for r in range(0, group, 2):
        got = feed(offsets, [hiddens[r], hiddens[r + 1]], [cots[r], cots[r + 1]], pieces, down)
        products.append(got[0])
        grads.append(got[1])
        terms_out[r], terms_out[r + 1], terms_back[r], terms_back[r + 1] = got[2:]
    hiddens = [hiddens[r] for r in range(group)]
    cots = [cots[r] for r in range(group)]
    total = lax.axis_size("dp")
    depth = total.bit_length() - 1
    levels = group.bit_length() - 1
    line = Line()
    count = inner // FB
    cuts = [0, -(-count // 2), count]
    share = 2 * slice_d // total
    order = jnp.stack(order).astype(jnp.int32)
    which = fast.astype(jnp.int32)[None]

    back = steps_of_scatter(terms_back, "seq")
    next(back)
    half_rows = slice_f // 2
    down_at = shift + half_rows * jnp.stack([fast, 1 - fast])
    down_keep, down_send = grad_down_of(products, cots, down_at.astype(jnp.int32), half_rows, [])
    down_steps = steps_of_sum(line, down_keep, down_send, 1, last=F32)
    next(down_steps)
    for _ in range(levels - 1):
        next(back)
    back_mine, back_got = next(back)
    first_keep, first_send, turned = grad_gate_up_of(
        grads, hiddens, 0, cuts[1], which, [down_keep, back_mine]
    )
    second_keep, second_send = grad_gate_up_of(
        grads, [turned], cuts[1], count - cuts[1], slow[None], []
    )
    f32 = lambda *shape: jax.ShapeDtypeStruct(shape, F32)
    bf16 = lambda *shape: jax.ShapeDtypeStruct(shape, BF16)

    grad_residual, grad_mixed, grad_gain_two = single_call(
        lambda _, *refs: residual_back_kernel(*refs), "norm_back",
        (back_mine, back_got, cot, residual, gain_two, full_out), [second_keep],
        [f32(rows, width), bf16(rows, width), f32(1, width)],
    )
    line.mark(grad_mixed)
    next(down_steps)
    first_steps = steps_of_sum(line, first_keep, first_send, group, order)
    next(first_steps)
    second_steps = steps_of_sum(line, second_keep, second_send, group, order, bits=[*range(1, depth), 0])
    next(second_steps)
    dq, *dkv = attention_backward(
        bounds, qt, ot, lse, grad_mixed, cos_t, sin_t, start_row, blocks, line.last
    )
    line.mark(dq)
    dkv_steps = steps_of_scatter(dict(enumerate(dkv)), "seq")
    next(dkv_steps)
    for _ in range(levels - 1):
        next(dkv_steps)
    next(second_steps)
    next(down_steps)
    dkv_mine, dkv_got = next(dkv_steps)
    qkv_width = w_qkv.shape[1]
    joint_width = qkv_width + width
    extra = -slice_d % (8 * total) or 8 * total
    joint_rows = slice_d + extra
    weights = [bf16(joint_rows, joint_width)] * group if aligned else [bf16(width, joint_width)]
    grad_inputs, grad_gain_one, grad_bias, *joint = single_call(
        functools.partial(project_back_kernel, aligned), "project_back",
        (tokens[0], gain_one, hidden_one, dq, dkv_mine, dkv_got, full_qkv, grad_residual, mixed, cos_k, sin_k),
        line.last,
        [f32(rows, width), f32(1, width), f32(1, qkv_width), *weights,
         pltpu.VMEM((rows, qkv_width), BF16), pltpu.VMEM((width, joint_width), BF16)],
        order * slice_d,
    )

    rest = jnp.concatenate(
        [
            grad_gain_one.reshape(group, slice_d),
            grad_gain_two.reshape(group, slice_d),
            grad_bias.reshape(group, slice_b),
        ],
        axis=1,
    ).astype(BF16)
    rest = jnp.pad(rest[:, None, :], ((0, 0), (0, 0), (0, joint_width - rest.shape[1])))
    if not aligned:
        joint = [
            jnp.pad(lax.dynamic_slice_in_dim(joint[0], order[r] * slice_d, slice_d, 0), ((0, extra), (0, 0)))
            for r in range(group)
        ]
    joint = {
        r: lax.dynamic_update_slice_in_dim(v, pick(rest, order[r]), slice_d, 0) for r, v in enumerate(joint)
    }
    line.last = [*line.last, grad_inputs]
    joint_steps = steps_of_scatter(joint, "seq")
    next(joint_steps)
    next(first_steps)
    next(second_steps)
    next(down_steps)
    for _ in range(levels - 1):
        next(joint_steps)
    next(first_steps)
    next(second_steps)
    next(down_steps)
    joint_mine, joint_got = next(joint_steps)
    keep, send = add_split(joint_mine, joint_got, 1, which[0], line.last)
    line.mark(keep)
    joint_steps = steps_of_sum(line, keep[0], send[0], 1, last=F32)
    next(joint_steps)
    next(second_steps)
    next(first_steps)
    out_steps = steps_of_scatter(terms_out, "seq")
    next(out_steps)
    next(second_steps)
    for _ in range(2 * (depth - 3)):
        for steps in (down_steps, first_steps, second_steps, joint_steps):
            next(steps)
    next(first_steps)
    next(joint_steps)
    next(down_steps)
    next(second_steps)
    next(joint_steps)
    next(first_steps)
    for _ in range(levels - 1):
        next(out_steps)
    next(joint_steps)
    down_sum = next(down_steps).reshape(slice_f, width)
    next(first_steps)
    second = next(second_steps)
    next(joint_steps)
    out_mine, out_got = next(out_steps)
    layer_out = (residual + out_mine.astype(F32) + out_got.astype(F32)).astype(BF16)
    next(joint_steps)
    first = next(first_steps)
    joint = next(joint_steps).reshape(joint_rows, joint_width)
    rest = joint[slice_d]
    lows, highs = [], []
    for i, done in enumerate((first, second)):
        columns = done.shape[-1]
        for kept, v in zip((lows, highs), done):
            v = jnp.moveaxis(v, depth - 1, 0).reshape(group, slice_d, columns)
            kept.append((cuts[i] * FB, v))
    gate_sum = join(lows, firsts, hidden_units)
    up_sum = join(highs, firsts, hidden_units)
    return (
        layer_out[None],
        grad_inputs[None],
        rest[:slice_d],
        joint[:slice_d, :qkv_width],
        rest[2 * slice_d : 2 * slice_d + slice_b],
        joint[:slice_d, qkv_width:],
        rest[slice_d : 2 * slice_d],
        gate_sum,
        up_sum,
        down_sum,
    )


def solution(mesh):
    return jax.shard_map(
        per_device,
        mesh=mesh,
        in_specs=(
            P("dp", "seq", None),
            P("dp", None),
            P("dp", "seq", None),
            P("seq"),
            P("seq", None),
            P("seq"),
            P("seq", None),
            P("seq"),
            P("seq", None),
            P("seq", None),
            P("seq", None),
        ),
        out_specs=(
            P("dp", "seq", None),
            P("dp", "seq", None),
            P("seq"),
            P("seq", None),
            P("seq"),
            P("seq", None),
            P("seq"),
            P("seq", None),
            P("seq", None),
            P("seq", None),
        ),
        check_vma=False,
    )
```

```python
import functools

import jax
import jax.numpy as jnp
from jax import lax
from jax.experimental import pallas as pl
from jax.experimental.pallas import tpu as pltpu
from jax.sharding import PartitionSpec as P

HEADS = 14
KV_HEADS = 2
HEAD_DIM = 64
GROUP = HEADS // KV_HEADS
EPSILON = 1e-06
ROPE_BASE = 1000000.0
SCALE = HEAD_DIM ** (-0.5)
QB = 128
KB = 256
BF16 = jnp.bfloat16
F32 = jnp.float32


def dot_rows(left, right):
    return lax.dot_general(left, right, (((0,), (0,)), ((), ())), preferred_element_type=F32)


def dot_last(left, right):
    return lax.dot_general(left, right, (((1,), (1,)), ((), ())), preferred_element_type=F32)


def dot(left, right):
    return jnp.dot(left, right, preferred_element_type=F32)


def swap(x, axis, mask):
    return lax.ppermute(x, axis, [(i, i ^ mask) for i in range(lax.axis_size(axis))])


def after(x, *deps):
    return lax.optimization_barrier((x, *deps))[0]


def pick(x, index):
    return lax.dynamic_index_in_dim(x, index, 0, keepdims=False)


def bits_down(n):
    bits = []
    b = n // 2
    while b:
        bits.append(b)
        b //= 2
    return bits


def gather_rel(x, axis):
    blocks = {0: x}
    for b in bits_down(lax.axis_size(axis)):
        blocks.update({r ^ b: swap(v, axis, b) for r, v in list(blocks.items())})
    return blocks


def scatter_rel(parts, axis):
    parts = dict(parts)
    for b in reversed(bits_down(lax.axis_size(axis))):
        kept = {}
        for r in [r for r in parts if not r & b]:
            kept[r] = (parts[r].astype(F32) + swap(parts[r ^ b], axis, b).astype(F32)).astype(BF16)
        parts = kept
    return parts[0]


def place(blocks, index):
    rows = blocks[0].shape[0]
    out = jnp.zeros((rows * len(blocks),) + blocks[0].shape[1:], blocks[0].dtype)
    for r, v in blocks.items():
        out = lax.dynamic_update_slice_in_dim(out, v, (index ^ r) * rows, 0)
    return out


def masks(start_ref, first_query, first_key):
    key = first_key + lax.broadcasted_iota(jnp.int32, (KB, QB), 0)
    query = first_query + lax.broadcasted_iota(jnp.int32, (KB, QB), 1)
    fine = (key >= start_ref[...]) & (key <= query)
    bias = jnp.where(fine, 0.0, -1e30).astype(F32)
    return jnp.concatenate([bias] * GROUP, axis=1)


def collect(bounds, blocks, k_ref, v_ref):
    me = bounds[bounds.shape[0] - 1]
    for r, block in enumerate(blocks):
        rows = block.shape[0]
        at = pl.multiple_of((me ^ r) * rows, QB)
        k_ref[pl.ds(at, rows), :] = block[:, : 2 * HEAD_DIM]
        v_ref[pl.ds(at, rows), :] = block[:, 2 * HEAD_DIM :]


def turn_over(source, target):
    for at in range(0, source.shape[0], QB):
        target[:, at : at + QB] = source[at : at + QB, :].astype(F32).T.astype(BF16)


def forward_kernel(group, bounds, pq_ref, cos_ref, sin_ref, start_ref, *rest):
    blocks = rest[:group]
    o_ref, qt_ref, ot_ref, lse_ref, qpad, top, total, acc, k_ref, v_ref, vt_ref = rest[-11:]
    b = pl.program_id(0)

    @pl.when(b == 0)
    def _():
        collect(bounds, blocks, k_ref, v_ref)
        turn_over(v_ref, vt_ref)

    lo, hi, first = bounds[3 * b], bounds[3 * b + 1], bounds[3 * b + 2]
    half = HEAD_DIM // 2
    turned = pq_ref[...].T
    cosine, sine = cos_ref[...], sin_ref[...]
    qpad[...] = jnp.zeros_like(qpad)
    for h in range(HEADS):
        g, i = divmod(h, GROUP)
        u1 = turned[h * HEAD_DIM : h * HEAD_DIM + half]
        u2 = turned[h * HEAD_DIM + half : (h + 1) * HEAD_DIM]
        both = jnp.concatenate([u1 * cosine - u2 * sine, u2 * cosine + u1 * sine], axis=0)
        both = both.astype(BF16) * jnp.asarray(SCALE, BF16)
        qpad[g, g * HEAD_DIM : (g + 1) * HEAD_DIM, i * QB : (i + 1) * QB] = both
        qt_ref[0, g, :, i * QB : (i + 1) * QB] = both
    top[...] = jnp.full_like(top, -1e30)
    total[...] = jnp.zeros_like(total)
    acc[...] = jnp.zeros_like(acc)

    def step(j, _):
        at = pl.multiple_of(j * KB, KB)
        keys = k_ref[pl.ds(at, KB), :]
        bias = masks(start_ref, first, at)
        for g in range(KV_HEADS):
            scores = dot(keys, qpad[g]) + bias
            new_top = jnp.maximum(top[g], jnp.max(scores, axis=0, keepdims=True))
            weights = jnp.exp(scores - new_top)
            fade = jnp.exp(top[g] - new_top)
            total[g] = total[g] * fade + jnp.sum(weights, axis=0, keepdims=True)
            values = vt_ref[g * HEAD_DIM : (g + 1) * HEAD_DIM, pl.ds(at, KB)]
            acc[g] = acc[g] * fade + dot(values, weights.astype(BF16))
            top[g] = new_top
        return 0

    lax.fori_loop(lo, hi, step, 0)
    pieces = []
    for g in range(KV_HEADS):
        mixed = acc[g] / total[g]
        ot_ref[0, g] = mixed.astype(BF16)
        lse_ref[0, g] = top[g] + jnp.log(total[g])
        pieces += [mixed[:, i * QB : (i + 1) * QB] for i in range(GROUP)]
    o_ref[...] = jnp.concatenate(pieces, axis=0).T.astype(BF16)


def backward_kernel(
    group, waits, bounds, qt_ref, ot_ref, lse_ref, do_ref, cos_ref, sin_ref, start_ref, *rest
):
    blocks, rest = rest[:group], rest[group + waits :]
    dq_ref, dkv_refs, rest = rest[0], rest[1 : 1 + group], rest[1 + group :]
    qpad, dopad, qrow, dorow, centre, dqt, dk_acc, dv_acc, k_ref, v_ref, kt_ref = rest
    b = pl.program_id(0)
    lo, hi, first = bounds[3 * b], bounds[3 * b + 1], bounds[3 * b + 2]
    half = HEAD_DIM // 2

    @pl.when(b == 0)
    def _():
        dk_acc[...] = jnp.zeros_like(dk_acc)
        dv_acc[...] = jnp.zeros_like(dv_acc)
        collect(bounds, blocks, k_ref, v_ref)
        turn_over(k_ref, kt_ref)

    qpad[...] = jnp.zeros_like(qpad)
    dopad[...] = jnp.zeros_like(dopad)
    dqt[...] = jnp.zeros_like(dqt)
    grads = do_ref[...].astype(F32)
    turned = grads.T
    lane = lax.broadcasted_iota(jnp.int32, (QB, 2 * HEAD_DIM), 1)
    for h in range(HEADS):
        g, i = divmod(h, GROUP)
        rows = slice(g * HEAD_DIM, (g + 1) * HEAD_DIM)
        cols = slice(i * QB, (i + 1) * QB)
        grad_t = turned[h * HEAD_DIM : (h + 1) * HEAD_DIM]
        dopad[g, rows, cols] = grad_t.astype(BF16)
        centre[g, :, cols] = jnp.sum(grad_t * ot_ref[0, g, :, cols].astype(F32), axis=0, keepdims=True)
        query_t = qt_ref[0, g, :, cols]
        qpad[g, rows, cols] = query_t
        mine = (lane >= g * HEAD_DIM) & (lane < (g + 1) * HEAD_DIM)
        pair = grads[:, (h // 2) * 2 * HEAD_DIM : (h // 2 + 1) * 2 * HEAD_DIM]
        if h % 2 != g:
            pair = pltpu.roll(pair, HEAD_DIM, 1)
        dorow[g, cols, :] = jnp.where(mine, pair, 0.0).astype(BF16)
        wide = qpad[g, :, cols].astype(F32)
        qrow[g, cols, :] = wide.T.astype(BF16)

    def step(j, _):
        at = pl.multiple_of(j * KB, KB)
        keys = k_ref[pl.ds(at, KB), :]
        values = v_ref[pl.ds(at, KB), :]
        bias = masks(start_ref, first, at)
        dk_term = None
        dv_term = None
        for g in range(KV_HEADS):
            probs = jnp.exp(dot(keys, qpad[g]) + bias - lse_ref[0, g])
            grad_probs = dot(values, dopad[g])
            grad_scores = (probs * (grad_probs - centre[g])).astype(BF16)
            dv_g = dot(probs.astype(BF16), dorow[g])
            dk_g = dot(grad_scores, qrow[g])
            dk_term = dk_g if g == 0 else dk_term + dk_g
            dv_term = dv_g if g == 0 else dv_term + dv_g
            turned_keys = kt_ref[g * HEAD_DIM : (g + 1) * HEAD_DIM, pl.ds(at, KB)]
            dqt[g] += dot(turned_keys, grad_scores)
        dk_acc[pl.ds(at, KB), :] += dk_term
        dv_acc[pl.ds(at, KB), :] += dv_term
        return 0

    lax.fori_loop(lo, hi, step, 0)
    cosine, sine = cos_ref[...], sin_ref[...]
    pieces = []
    for h in range(HEADS):
        g, i = divmod(h, GROUP)
        w1 = dqt[g, :half, i * QB : (i + 1) * QB] * SCALE
        w2 = dqt[g, half:, i * QB : (i + 1) * QB] * SCALE
        pieces += [w1 * cosine + w2 * sine, w2 * cosine - w1 * sine]
    dq_ref[...] = jnp.concatenate(pieces, axis=0).T.astype(BF16)

    @pl.when(b == pl.num_programs(0) - 1)
    def _():
        me = bounds[bounds.shape[0] - 1]
        for r, ref in enumerate(dkv_refs):
            rows = ref.shape[0]
            at = pl.multiple_of((me ^ r) * rows, QB)
            ref[:, : 2 * HEAD_DIM] = dk_acc[pl.ds(at, rows), :].astype(BF16)
            ref[:, 2 * HEAD_DIM :] = dv_acc[pl.ds(at, rows), :].astype(BF16)


def whole(shape):
    return pl.BlockSpec(shape, lambda b, *_: (0,) * len(shape))


def attention_forward(bounds, pq, cos_t, sin_t, start, blocks, waits):
    rows = pq.shape[0]
    length = rows * len(blocks)
    count = rows // QB
    width = HEADS * HEAD_DIM
    lanes = GROUP * QB
    return pl.pallas_call(
        functools.partial(forward_kernel, len(blocks)),
        out_shape=(
            jax.ShapeDtypeStruct((rows, width), BF16),
            jax.ShapeDtypeStruct((count, KV_HEADS, HEAD_DIM, lanes), BF16),
            jax.ShapeDtypeStruct((count, KV_HEADS, HEAD_DIM, lanes), BF16),
            jax.ShapeDtypeStruct((count, KV_HEADS, 1, lanes), F32),
        ),
        grid_spec=pltpu.PrefetchScalarGridSpec(
            num_scalar_prefetch=1,
            grid=(count,),
            in_specs=[
                pl.BlockSpec((QB, width), lambda b, *_: (b, 0)),
                pl.BlockSpec((HEAD_DIM // 2, QB), lambda b, *_: (0, b)),
                pl.BlockSpec((HEAD_DIM // 2, QB), lambda b, *_: (0, b)),
                pl.BlockSpec((1, QB), lambda b, *_: (0, b)),
                *[whole((rows, 4 * HEAD_DIM))] * len(blocks),
                *[pl.BlockSpec(memory_space=pl.ANY)] * len(waits),
            ],
            out_specs=[
                pl.BlockSpec((QB, width), lambda b, *_: (b, 0)),
                pl.BlockSpec((1, KV_HEADS, HEAD_DIM, lanes), lambda b, *_: (b, 0, 0, 0)),
                pl.BlockSpec((1, KV_HEADS, HEAD_DIM, lanes), lambda b, *_: (b, 0, 0, 0)),
                pl.BlockSpec((1, KV_HEADS, 1, lanes), lambda b, *_: (b, 0, 0, 0)),
            ],
            scratch_shapes=[
                pltpu.VMEM((KV_HEADS, 2 * HEAD_DIM, lanes), BF16),
                pltpu.VMEM((KV_HEADS, 1, lanes), F32),
                pltpu.VMEM((KV_HEADS, 1, lanes), F32),
                pltpu.VMEM((KV_HEADS, HEAD_DIM, lanes), F32),
                pltpu.VMEM((length, 2 * HEAD_DIM), BF16),
                pltpu.VMEM((length, 2 * HEAD_DIM), BF16),
                pltpu.VMEM((2 * HEAD_DIM, length), BF16),
            ],
        ),
        compiler_params=pltpu.CompilerParams(vmem_limit_bytes=40 << 20),
        cost_estimate=pl.CostEstimate(
            flops=1 << 22, bytes_accessed=1 << 18, transcendentals=0
        ),
        name="attention_forward",
    )(bounds, pq, cos_t, sin_t, start, *blocks, *waits)


def attention_backward(bounds, qt, ot, lse, grad_mixed, cos_t, sin_t, start, blocks, waits):
    rows = grad_mixed.shape[0]
    group = len(blocks)
    length = rows * group
    count = rows // QB
    width = HEADS * HEAD_DIM
    lanes = GROUP * QB
    return pl.pallas_call(
        functools.partial(backward_kernel, group, len(waits)),
        out_shape=(
            jax.ShapeDtypeStruct((rows, width), BF16),
            *[jax.ShapeDtypeStruct((rows, 4 * HEAD_DIM), BF16)] * group,
        ),
        grid_spec=pltpu.PrefetchScalarGridSpec(
            num_scalar_prefetch=1,
            grid=(count,),
            in_specs=[
                pl.BlockSpec((1, KV_HEADS, HEAD_DIM, lanes), lambda b, *_: (b, 0, 0, 0)),
                pl.BlockSpec((1, KV_HEADS, HEAD_DIM, lanes), lambda b, *_: (b, 0, 0, 0)),
                pl.BlockSpec((1, KV_HEADS, 1, lanes), lambda b, *_: (b, 0, 0, 0)),
                pl.BlockSpec((QB, width), lambda b, *_: (b, 0)),
                pl.BlockSpec((HEAD_DIM // 2, QB), lambda b, *_: (0, b)),
                pl.BlockSpec((HEAD_DIM // 2, QB), lambda b, *_: (0, b)),
                pl.BlockSpec((1, QB), lambda b, *_: (0, b)),
                *[whole((rows, 4 * HEAD_DIM))] * group,
                *[pl.BlockSpec(memory_space=pl.ANY)] * len(waits),
            ],
            out_specs=[
                pl.BlockSpec((QB, width), lambda b, *_: (b, 0)),
                *[whole((rows, 4 * HEAD_DIM))] * group,
            ],
            scratch_shapes=[
                pltpu.VMEM((KV_HEADS, 2 * HEAD_DIM, lanes), BF16),
                pltpu.VMEM((KV_HEADS, 2 * HEAD_DIM, lanes), BF16),
                pltpu.VMEM((KV_HEADS, lanes, 2 * HEAD_DIM), BF16),
                pltpu.VMEM((KV_HEADS, lanes, 2 * HEAD_DIM), BF16),
                pltpu.VMEM((KV_HEADS, 1, lanes), F32),
                pltpu.VMEM((KV_HEADS, HEAD_DIM, lanes), F32),
                pltpu.VMEM((length, 2 * HEAD_DIM), F32),
                pltpu.VMEM((length, 2 * HEAD_DIM), F32),
                pltpu.VMEM((length, 2 * HEAD_DIM), BF16),
                pltpu.VMEM((length, 2 * HEAD_DIM), BF16),
                pltpu.VMEM((2 * HEAD_DIM, length), BF16),
            ],
        ),
        compiler_params=pltpu.CompilerParams(vmem_limit_bytes=48 << 20),
        cost_estimate=pl.CostEstimate(
            flops=1 << 22, bytes_accessed=1 << 18, transcendentals=0
        ),
        name="attention_backward",
    )(bounds, qt, ot, lse, grad_mixed, cos_t, sin_t, start, *blocks, *waits)


def project_kernel(offsets, x_ref, gain_ref, bias_ref, cos_ref, sin_ref, *rest):
    pieces = rest[:-6]
    pass_ref, q_ref, kv_ref, hidden_ref, w_ref, passed_ref = rest[-6:]
    passed_ref[...] = pass_ref[...]
    for i, piece in enumerate(pieces):
        count = piece.shape[0]
        w_ref[pl.ds(pl.multiple_of(offsets[i], 16), count), :] = piece[...]
    x = x_ref[...].astype(F32)
    scale = lax.rsqrt(jnp.mean(x * x, axis=-1, keepdims=True) + EPSILON)
    hidden = (x * scale * gain_ref[...]).astype(BF16)
    hidden_ref[...] = hidden
    query_width = HEADS * HEAD_DIM
    key_width = KV_HEADS * HEAD_DIM
    q_ref[...] = dot(hidden, w_ref[:, :query_width]) + bias_ref[:, :query_width]
    kv = dot(hidden, w_ref[:, query_width:]) + bias_ref[:, query_width:]
    keys = kv[:, :key_width]
    lane = lax.broadcasted_iota(jnp.int32, keys.shape, 1) % HEAD_DIM
    half = HEAD_DIM // 2
    other = jnp.where(
        lane < half, pltpu.roll(keys, key_width - half, 1), pltpu.roll(keys, half, 1)
    )
    keys = keys * cos_ref[...] + other * sin_ref[...]
    kv_ref[:, :key_width] = keys.astype(BF16)
    kv_ref[:, key_width:] = kv[:, key_width:].astype(BF16)


def project(offsets, x, gain, bias, cosine, sine, pieces, passed):
    rows, width = x.shape
    total = bias.shape[1]
    query_width = HEADS * HEAD_DIM
    return pl.pallas_call(
        project_kernel,
        out_shape=(
            jax.ShapeDtypeStruct((rows, query_width), F32),
            jax.ShapeDtypeStruct((rows, total - query_width), BF16),
            jax.ShapeDtypeStruct((rows, width), BF16),
            jax.ShapeDtypeStruct((width, total), BF16),
            jax.ShapeDtypeStruct(passed.shape, BF16),
        ),
        grid_spec=pltpu.PrefetchScalarGridSpec(
            num_scalar_prefetch=1,
            grid=(1,),
            in_specs=[whole(v.shape) for v in (x, gain, bias, cosine, sine, *pieces, passed)],
            out_specs=[
                whole((rows, query_width)),
                whole((rows, total - query_width)),
                whole((rows, width)),
                whole((width, total)),
                whole(passed.shape),
            ],
        ),
        compiler_params=pltpu.CompilerParams(vmem_limit_bytes=40 << 20),
        cost_estimate=pl.CostEstimate(
            flops=2 * rows * width * total, bytes_accessed=8 << 20, transcendentals=0
        ),
        name="norm_project_rotate",
    )(offsets, x, gain, bias, cosine, sine, *pieces, passed)


def output_kernel(pieces, offsets, x_ref, mixed_ref, gain_ref, *rest):
    residual_ref, hidden_ref, w_ref = rest[-3:]
    for i, piece in enumerate(rest[:pieces]):
        w_ref[pl.ds(pl.multiple_of(offsets[i], 16), piece.shape[0]), :] = piece[...]
    residual = x_ref[...].astype(F32) + dot(mixed_ref[...], w_ref[...])
    residual_ref[...] = residual
    scale = lax.rsqrt(jnp.mean(residual * residual, axis=-1, keepdims=True) + EPSILON)
    hidden_ref[...] = (residual * scale * gain_ref[...]).astype(BF16)


def output_of(offsets, x, mixed, gain, pieces, waits):
    rows, width = x.shape
    return pl.pallas_call(
        functools.partial(output_kernel, len(pieces)),
        out_shape=(
            jax.ShapeDtypeStruct((rows, width), F32),
            jax.ShapeDtypeStruct((rows, width), BF16),
            jax.ShapeDtypeStruct((width, width), BF16),
        ),
        grid_spec=pltpu.PrefetchScalarGridSpec(
            num_scalar_prefetch=1,
            grid=(1,),
            in_specs=[
                *[whole(v.shape) for v in (x, mixed, gain, *pieces)],
                *[pl.BlockSpec(memory_space=pl.ANY)] * len(waits),
            ],
            out_specs=[whole((rows, width)), whole((rows, width)), whole((width, width))],
        ),
        compiler_params=pltpu.CompilerParams(vmem_limit_bytes=40 << 20),
        cost_estimate=pl.CostEstimate(flops=1 << 22, bytes_accessed=1 << 18, transcendentals=0),
        name="project_add_norm",
    )(offsets, x, mixed, gain, *pieces, *waits)


FB = 256


def feed_kernel(blocks, offsets, *refs):
    hs, dys, refs = refs[:blocks], refs[blocks : 2 * blocks], refs[2 * blocks :]
    count = offsets.shape[0]
    pieces, refs = refs[:count], refs[count:]
    wd_ref, m_ref, d_ref = refs[:3]
    outs, backs = refs[3 : 3 + blocks], refs[3 + blocks : 3 + 2 * blocks]
    out_acc, dh_acc, wg, wu = refs[3 + 2 * blocks :]
    step = pl.program_id(0)
    last = pl.num_programs(0) - 1
    rows = hs[0].shape[0]
    for i, piece in enumerate(pieces):
        at = pl.ds(pl.multiple_of(offsets[i], 16), piece.shape[1])
        wg[at, :] = piece[0]
        wu[at, :] = piece[1]

    @pl.when(step == 0)
    def _():
        out_acc[...] = jnp.zeros_like(out_acc)
        dh_acc[...] = jnp.zeros_like(dh_acc)

    for t in range(blocks):
        at = slice(t * rows, (t + 1) * rows)
        hidden, cot = hs[t][...], dys[t][...]
        gate = dot(hidden, wg[...])
        upward = dot(hidden, wu[...])
        grad_product = dot_last(cot, wd_ref[...])
        sigma = jax.nn.sigmoid(gate)
        active = gate * sigma
        product = (active * upward).astype(BF16)
        grad_gate = (grad_product * upward * (sigma + active * (1.0 - sigma))).astype(BF16)
        grad_up = (grad_product * active).astype(BF16)
        d_ref[0, at], d_ref[1, at] = grad_gate, grad_up
        m_ref[:, at] = (active * upward).T.astype(BF16)
        out_acc[at] += dot(product, wd_ref[...])
        dh_acc[at] += dot_last(grad_gate, wg[...]) + dot_last(grad_up, wu[...])

    @pl.when(step == last)
    def _():
        for t in range(blocks):
            at = slice(t * rows, (t + 1) * rows)
            outs[t][...] = out_acc[at].astype(BF16)
            backs[t][...] = dh_acc[at].astype(BF16)


def feed(offsets, hiddens, cots, pieces, w_down):
    blocks = len(hiddens)
    rows, width = hiddens[0].shape
    inner = w_down.shape[0]
    wide = jax.ShapeDtypeStruct((2, blocks * rows, inner), BF16)
    tall = jax.ShapeDtypeStruct((inner, blocks * rows), BF16)
    narrow = jax.ShapeDtypeStruct((rows, width), BF16)
    return pl.pallas_call(
        functools.partial(feed_kernel, blocks),
        out_shape=(tall, wide) + (narrow,) * (2 * blocks),
        grid_spec=pltpu.PrefetchScalarGridSpec(
            num_scalar_prefetch=1,
            grid=(inner // FB,),
            in_specs=[
                *[whole((rows, width))] * (2 * blocks),
                *[pl.BlockSpec((2, v.shape[1], FB), lambda j, *_: (0, 0, j)) for v in pieces],
                pl.BlockSpec((FB, width), lambda j, *_: (j, 0)),
            ],
            out_specs=[
                pl.BlockSpec((FB, blocks * rows), lambda j, *_: (j, 0)),
                pl.BlockSpec((2, blocks * rows, FB), lambda j, *_: (0, 0, j)),
                *[whole((rows, width))] * (2 * blocks),
            ],
            scratch_shapes=[
                pltpu.VMEM((blocks * rows, width), F32),
                pltpu.VMEM((blocks * rows, width), F32),
                pltpu.VMEM((width, FB), BF16),
                pltpu.VMEM((width, FB), BF16),
            ],
        ),
        compiler_params=pltpu.CompilerParams(vmem_limit_bytes=48 << 20),
        cost_estimate=pl.CostEstimate(
            flops=1 << 22, bytes_accessed=1 << 18, transcendentals=0
        ),
        name="feed_forward_backward",
    )(offsets, *hiddens, *cots, *pieces, w_down)


def down_kernel(parts, per, cut, offsets, *refs):
    ms, dys, outs = refs[:parts], refs[parts : parts + parts * per], refs[-2:]
    for k, out_ref in enumerate(outs):
        rows = out_ref.shape[0]

        @pl.when(pl.program_id(0) == 1 - k)
        def _():
            total = None
            for i, m_ref in enumerate(ms):
                width = m_ref.shape[-1] // per
                for t in range(per):
                    if cut:
                        at = pl.ds(pl.multiple_of(offsets[k], 16), rows)
                        left = m_ref[at, t * width : (t + 1) * width]
                    else:
                        left = m_ref[k, :, t * width : (t + 1) * width]
                    term = dot(left, dys[i * per + t][...])
                    total = term if total is None else total + term
            out_ref[...] = total.astype(BF16)


def grad_down_of(products, cots, offsets, half, waits):
    rows, width = cots[0].shape
    cut = half % 16 == 0
    if not cut:
        products = [
            jnp.stack([lax.dynamic_slice_in_dim(v, offsets[k], half, 0) for k in range(2)]) for v in products
        ]
    out = jax.ShapeDtypeStruct((half, width), BF16)
    return pl.pallas_call(
        functools.partial(down_kernel, len(products), len(cots) // len(products), cut),
        out_shape=(out, out),
        grid_spec=pltpu.PrefetchScalarGridSpec(
            num_scalar_prefetch=1,
            grid=(2,),
            in_specs=[*[whole(v.shape) for v in (*products, *cots)], *[ANY] * len(waits)],
            out_specs=[whole((half, width))] * 2,
        ),
        compiler_params=pltpu.CompilerParams(vmem_limit_bytes=56 << 20),
        cost_estimate=pl.CostEstimate(flops=1 << 22, bytes_accessed=1 << 18, transcendentals=0),
        name="grad_down",
    )(offsets, *products, *cots, *waits)


def gate_up_kernel(parts, blocks, total, *refs):
    grads, hs, (out, turned) = refs[:parts], refs[parts : parts + blocks], refs[-2:]
    groups, share = out.shape[1:3]
    each = turned.shape[0] // groups

    @pl.when(pl.program_id(0) == 0)
    def _():
        rows = hs[0].shape[0]
        for t, h in enumerate(hs):
            for at in range(0, rows, QB):
                place_at = slice(t * rows + at, t * rows + at + QB)
                turned[:, place_at] = h[at : at + QB, :].astype(F32).T.astype(BF16)

    for i in range(2):
        result = None
        first = 0
        for v in grads:
            term = dot(turned[:, first : first + v.shape[1]], v[i])
            result = term if result is None else result + term
            first += v.shape[1]
        for k in range(total // 2):
            for j in range(groups):
                at = j * each + turned_bits(k, total // 2) * share
                out[2 * k + i, j] = result[at : at + share].astype(BF16)


def turned_bits(k, count):
    out = 0
    while count > 1:
        out, k, count = out * 2 + k % 2, k // 2, count // 2
    return out


def grad_gate_up_of(grads, hiddens, groups, total, waits):
    width = hiddens[0].shape[1]
    tokens = sum(v.shape[1] for v in grads)
    inner = grads[0].shape[2]
    share = 2 * width // (groups * total)
    return pl.pallas_call(
        functools.partial(gate_up_kernel, len(grads), len(hiddens), total),
        out_shape=jax.ShapeDtypeStruct((total, groups, share, inner), BF16),
        grid=(inner // FB,),
        in_specs=[
            *[pl.BlockSpec((2, v.shape[1], FB), lambda j: (0, 0, j)) for v in grads],
            *[whole(v.shape) for v in hiddens],
            *[ANY] * len(waits),
        ],
        out_specs=pl.BlockSpec((total, groups, share, FB), lambda j: (0, 0, 0, j)),
        scratch_shapes=[pltpu.VMEM((width, tokens), BF16)],
        compiler_params=pltpu.CompilerParams(vmem_limit_bytes=56 << 20),
        cost_estimate=pl.CostEstimate(flops=1 << 22, bytes_accessed=1 << 18, transcendentals=0),
        name="grad_gate_up",
    )(*grads, *hiddens, *waits)


def residual_back_kernel(mine_ref, got_ref, cot_ref, residual_ref, gain_ref, w_ref, *rest):
    grad_ref, mixed_ref, gain_out = rest[-3:]
    grad_hidden = mine_ref[...].astype(F32) + got_ref[...].astype(F32)
    residual = residual_ref[...]
    scale = lax.rsqrt(jnp.mean(residual * residual, axis=-1, keepdims=True) + EPSILON)
    normed = residual * scale
    gain_out[...] = jnp.sum(grad_hidden * normed, axis=0, keepdims=True)
    grad = cot_ref[...].astype(F32) + norm_back(grad_hidden, normed, scale, gain_ref[...])
    grad_ref[...] = grad
    mixed_ref[...] = dot_last(grad.astype(BF16), w_ref[...]).astype(BF16)


def single_call(kernel, name, ins, waits, outs, scalars=None):
    scalars = jnp.zeros((1,), jnp.int32) if scalars is None else scalars
    scratch = [v for v in outs if isinstance(v, type(pltpu.VMEM((8, 128), F32)))]
    outs = [v for v in outs if v not in scratch]

    def body(scalar_ref, *refs):
        kernel(scalar_ref, *refs[: len(ins)], *refs[len(ins) + len(waits) :])

    return pl.pallas_call(
        body,
        out_shape=outs,
        grid_spec=pltpu.PrefetchScalarGridSpec(
            num_scalar_prefetch=1,
            grid=(1,),
            in_specs=[*[whole(v.shape) for v in ins], *[ANY] * len(waits)],
            out_specs=[whole(v.shape) for v in outs],
            scratch_shapes=scratch,
        ),
        compiler_params=pltpu.CompilerParams(vmem_limit_bytes=52 << 20),
        cost_estimate=pl.CostEstimate(flops=1 << 22, bytes_accessed=1 << 18, transcendentals=0),
        name=name,
    )(scalars, *ins, *waits)


def project_back_kernel(
    aligned, offsets, x_ref, gain_ref, hidden_ref, dq_ref, mine_ref, got_ref, w_ref, grad_ref, mixed_ref,
    cos_ref, sin_ref, out_ref, gain_out, bias_out, *rest
):
    weights, (dp_ref, dw_ref) = rest[:-2], rest[-2:]
    query_width = HEADS * HEAD_DIM
    key_width = KV_HEADS * HEAD_DIM
    half = HEAD_DIM // 2
    total = w_ref.shape[1]
    dkv = mine_ref[...].astype(F32) + got_ref[...].astype(F32)
    keys = dkv[:, :key_width]
    lane = lax.broadcasted_iota(jnp.int32, keys.shape, 1) % HEAD_DIM
    other = jnp.where(
        lane < half, pltpu.roll(keys, key_width - half, 1), pltpu.roll(keys, half, 1)
    )
    dp_ref[:, :query_width] = dq_ref[...]
    dp_ref[:, query_width : query_width + key_width] = (
        keys * cos_ref[...] - other * sin_ref[...]
    ).astype(BF16)
    dp_ref[:, query_width + key_width :] = dkv[:, key_width:].astype(BF16)
    grads = dp_ref[...]
    bias_out[...] = jnp.sum(grads.astype(F32), axis=0, keepdims=True)
    back = dot_last(grads, w_ref[...])
    x = x_ref[...].astype(F32)
    scale = lax.rsqrt(jnp.mean(x * x, axis=-1, keepdims=True) + EPSILON)
    normed = x * scale
    gain_out[...] = jnp.sum(back * normed, axis=0, keepdims=True)
    out_ref[...] = grad_ref[...] + norm_back(back, normed, scale, gain_ref[...])
    dw_ref[:, :total] = dot(hidden_ref[...].astype(F32).T.astype(BF16), grads).astype(BF16)
    dw_ref[:, total:] = dot(
        mixed_ref[...].astype(F32).T.astype(BF16), grad_ref[...].astype(BF16)
    ).astype(BF16)
    if aligned:
        rows = dw_ref.shape[0] // len(weights)
        for k, ref in enumerate(weights):
            ref[:rows] = dw_ref[pl.ds(pl.multiple_of(offsets[k], 16), rows), :]
            ref[rows:] = jnp.zeros((ref.shape[0] - rows, ref.shape[1]), BF16)
    else:
        weights[0][...] = dw_ref[...]


ANY = pl.BlockSpec(memory_space=pl.ANY)


class Line:
    def __init__(self):
        self.last = []

    def mark(self, x):
        self.last = [x]
        return x


def small_call(kernel, name, scalars, grid, ins, in_specs, out_shape, out_specs, waits):
    count = len(ins)

    def body(scalar_ref, *refs):
        kernel(scalar_ref, refs[:count], refs[count + len(waits) :])

    return pl.pallas_call(
        body,
        out_shape=out_shape,
        grid_spec=pltpu.PrefetchScalarGridSpec(
            num_scalar_prefetch=1,
            grid=grid,
            in_specs=[*in_specs, *[ANY] * len(waits)],
            out_specs=out_specs,
        ),
        compiler_params=pltpu.CompilerParams(vmem_limit_bytes=40 << 20),
        cost_estimate=pl.CostEstimate(flops=1 << 20, bytes_accessed=1 << 18, transcendentals=0),
        name=name,
    )(scalars, *ins, *waits)


def add_split(x, got, lead, mine, waits):
    columns = x.shape[-1]
    x, got = x.reshape(lead, 2, -1, columns), got.reshape(lead, 2, -1, columns)
    rows = x.shape[2]

    def kernel(_, ins, outs):
        for k in range(2):
            total = ins[2 * k][0, 0].astype(F32) + ins[2 * k + 1][0, 0].astype(F32)
            outs[k][0] = total.astype(BF16)

    keep = pl.BlockSpec((1, 1, rows, columns), lambda i, at: (i, at[0], 0, 0))
    send = pl.BlockSpec((1, 1, rows, columns), lambda i, at: (i, 1 - at[0], 0, 0))
    half = jax.ShapeDtypeStruct((lead, rows, columns), BF16)
    out = pl.BlockSpec((1, rows, columns), lambda i, at: (i, 0, 0))
    return small_call(
        kernel, "add_and_split", mine[None], (lead,), (x, got, x, got), (keep, keep, send, send),
        (half, half), (out, out), waits,
    )


def add_ordered(x, got, order, waits):
    shape = (1,) + x.shape[1:]
    got = got.reshape(x.shape)

    def kernel(_, ins, outs):
        for k, out in enumerate(outs):
            out[...] = (ins[2 * k][...].astype(F32) + ins[2 * k + 1][...].astype(F32)).astype(BF16)

    specs = []
    for k in range(order.shape[0]):
        specs += [pl.BlockSpec(shape, lambda i, at, k=k: (at[k], 0, 0))] * 2
    count = order.shape[0]
    return small_call(
        kernel, "add", order, (1,), (x, got) * count, specs,
        (jax.ShapeDtypeStruct(shape, BF16),) * count, (whole(shape),) * count, waits,
    )


def put_ordered(parts, order, waits, dtype=BF16):
    shape = parts[0].shape
    block = shape[-2:]
    lead = parts[0].size // (block[0] * block[1])
    parts = [v.reshape((lead,) + block) for v in parts]
    count = len(parts)

    def kernel(at, ins, outs):
        for k in range(count):
            outs[0][at[k]] = ins[k][...].astype(dtype)

    (out,) = small_call(
        kernel, "place", order, (lead,), parts,
        [pl.BlockSpec((1,) + block, lambda i, at: (i, 0, 0))] * count,
        (jax.ShapeDtypeStruct((count, lead) + block, dtype),),
        (pl.BlockSpec((count, 1) + block, lambda i, at: (0, i, 0, 0)),), waits,
    )
    return out.reshape((count,) + shape)


def steps_of_sum(line, keep, send):
    index = lax.axis_index("dp")
    depth = lax.axis_size("dp").bit_length() - 1
    bits = [((index >> k) & 1).astype(jnp.int32) for k in range(depth)]
    columns = keep.shape[-1]
    for k in range(depth - 1):
        got = swap(send, "dp", 1 << k)
        yield None
        keep, send = add_split(keep, got, 1, bits[k + 1], line.last)
        line.mark(keep)
    got = swap(send, "dp", 1 << (depth - 1))
    yield None
    part = line.mark(add(keep.reshape(1, -1, columns), got, line.last))
    yield from steps_of_gather(line, part, reversed(range(depth)))


def steps_of_gather(line, part, order):
    index = lax.axis_index("dp")
    order = list(order)
    for k in order:
        bit = ((index >> k) & 1).astype(jnp.int32)
        got = swap(part, "dp", 1 << k)
        yield None
        if k == order[-1]:
            yield jnp.where(bit == 0, part, got), jnp.where(bit == 0, got, part)
        part = line.mark(put_ordered([part, got], jnp.stack([bit, 1 - bit]), line.last))


def add(x, got, waits):
    return add_ordered(x, got, jnp.zeros((1,), jnp.int32), waits)[0]


def steps_of_scatter(parts, axis):
    parts = dict(parts)
    for b in reversed(bits_down(lax.axis_size(axis))):
        got = {r: swap(parts[r ^ b], axis, b) for r in parts if not r & b}
        yield None
        if len(got) == 1:
            yield parts[0], got[0]
        parts = {r: (parts[r].astype(F32) + v.astype(F32)).astype(BF16) for r, v in got.items()}


def pad_rows(x, multiple):
    extra = -x.shape[0] % multiple
    return jnp.pad(x, ((0, extra), (0, 0))) if extra else x


def locate(lengths, where_at):
    starts = jnp.cumsum(lengths) - lengths
    inside = where_at[:, None] >= starts[None, :]
    return jnp.max(jnp.where(inside, starts[None, :], 0), axis=1)


def norm_back(grad_hidden, normed, scale_rows, gain):
    scaled = grad_hidden * gain
    return scale_rows * (scaled - normed * jnp.mean(scaled * normed, axis=-1, keepdims=True))


def turn_heads(values, cosine, sine):
    rows = values.shape[0]
    values = values.reshape(rows, KV_HEADS, HEAD_DIM)
    half = HEAD_DIM // 2
    first, second = values[..., :half], values[..., half:]
    cosine, sine = cosine[:, None, :], sine[:, None, :]
    turned = jnp.concatenate([first * cosine - second * sine, second * cosine + first * sine], axis=-1)
    return turned.reshape(rows, KV_HEADS * HEAD_DIM)


def swaps(x, axis):
    return {r: swap(x, axis, r) if r else x for r in range(lax.axis_size(axis))}


def windows(total, count, tile=128):
    each = total // count
    firsts = [j * each // tile * tile for j in range(count)]
    width = max(j * each - first + each for j, first in enumerate(firsts))
    return -(-width // FB) * FB, firsts


def join(parts, firsts, total, tile=128):
    runs = []
    for at in range(0, total, tile):
        cover = []
        for i, (first, values) in enumerate(parts):
            for j, begin in enumerate(firsts):
                local = at - begin - first
                if 0 <= local < values.shape[-1]:
                    cover.append((i, j, local))
        if runs and [(i, j, c - runs[-1][1]) for i, j, c in cover] == runs[-1][0]:
            runs[-1][1] += tile
        else:
            runs.append([cover, tile])
    segments = []
    for cover, width in runs:
        segments.append(
            sum(parts[i][1][j, :, c : c + width].astype(F32) for i, j, c in cover)
        )
    return jnp.concatenate(segments, axis=1)


def per_device(
    tokens, doc_lengths, cotangent, norm_one, w_qkv, b_qkv, w_out, norm_two, w_gate, w_up, w_down
):
    group = lax.axis_size("seq")
    me = lax.axis_index("seq")
    inputs = tokens[0].astype(F32)
    rows, width = inputs.shape
    query_width = HEADS * HEAD_DIM
    key_width = KV_HEADS * HEAD_DIM
    slice_d = width // group
    slice_b = b_qkv.shape[0]
    slice_f = w_down.shape[0]
    hidden_units = slice_f * group
    aligned = slice_d % 32 == 0

    small = jnp.concatenate([norm_one, norm_two, b_qkv])[None, :]
    small = place(swaps(small, "seq"), me)
    gain_one = small[:, :slice_d].reshape(1, width).astype(F32)
    gain_two = small[:, slice_d : 2 * slice_d].reshape(1, width).astype(F32)
    bias = small[:, 2 * slice_d :].reshape(1, -1).astype(F32)
    pieces_qkv = gather_rel(w_qkv, "seq")
    order = [me ^ r for r in range(group)]
    if aligned:
        offsets_qkv = jnp.stack([j * slice_d for j in order]).astype(jnp.int32)
        pieces_qkv = [pieces_qkv[r] for r in range(group)]
    else:
        offsets_qkv = jnp.zeros((1,), jnp.int32)
        pieces_qkv = [place(pieces_qkv, me)]

    inner, firsts = windows(hidden_units, group)
    both = jnp.stack([w_gate, w_up])
    both = jnp.pad(both, ((0, 0), (0, 0), (0, max(0, firsts[-1] + inner - hidden_units))))
    both = jnp.stack([both[:, :, at : at + inner] for at in firsts])
    shift = lax.rem(me * slice_f, 128)
    down = lax.dynamic_update_slice_in_dim(jnp.zeros((inner, width), BF16), w_down, shift, 0)

    half_d = slice_d // 2
    fast = (lax.axis_index("dp") & 1).astype(jnp.int32)
    slow = ((lax.axis_index("dp") >> 1) & 1).astype(jnp.int32)
    early = {}
    for r in range(2, group):
        part = lax.dynamic_slice(
            both, (order[r], slow, fast * half_d, 0), (1, 1, half_d, inner)
        )
        early[r] = swap(part.reshape(half_d, inner), "seq", r)

    offset = me * rows
    index = offset + jnp.arange(rows, dtype=jnp.int32)
    start = locate(doc_lengths[0], index)
    places = (index - start).astype(F32)
    half = HEAD_DIM // 2
    freqs = ROPE_BASE ** (-(jnp.arange(half, dtype=F32) * 2.0) / HEAD_DIM)
    angle = places[:, None] * freqs[None, :]
    cosine, sine = jnp.cos(angle), jnp.sin(angle)
    cos_t, sin_t = cosine.T, sine.T
    cos_k = jnp.concatenate([cosine] * (2 * KV_HEADS), axis=1)
    sin_k = jnp.concatenate([-sine, sine] * KV_HEADS, axis=1)
    marks = offset + jnp.arange(rows // QB, dtype=jnp.int32) * QB
    bounds = jnp.stack([start[::QB] // KB, (marks + QB - 1) // KB + 1, marks], axis=1).reshape(-1)
    bounds = jnp.concatenate([bounds, me[None]]).astype(jnp.int32)
    start_row = start.astype(jnp.int32)[None, :]

    queries, kv, hidden_one, full_qkv, w_out = project(
        offsets_qkv, tokens[0], gain_one, bias, cos_k, sin_k, pieces_qkv, w_out
    )
    pieces_out = gather_rel(w_out, "seq")
    pieces_out = [pieces_out[r] for r in range(group)] if aligned else [place(pieces_out, me)]
    (kv,) = single_call(
        lambda _, a, b: b.__setitem__(..., a[...]), "pass_on", (kv,), [early[r] for r in early],
        [jax.ShapeDtypeStruct(kv.shape, BF16)],
    )
    blocks = gather_rel(kv, "seq")
    blocks = [blocks[r] for r in range(group)]
    later = {}
    pieces = [pick(both, order[0]), swap(pick(both, order[1]), "seq", 1)]
    offsets = [order[0] * slice_d, order[1] * slice_d]
    for r in range(2, group):
        got = swap(early[r], "dp", 2)
        later[r] = part = put_ordered([early[r], got], jnp.stack([slow, 1 - slow]), [])
        pieces += [part, swap(part, "dp", 1)]
        at = order[r] * slice_d
        offsets += [at + fast * half_d, at + (1 - fast) * half_d]
    if not aligned:
        full = jnp.zeros((2, width, inner), BF16)
        for piece, at in zip(pieces, offsets):
            full = lax.dynamic_update_slice(full, piece, (0, at, 0))
        pieces, offsets = [full], [0 * me]
    offsets = jnp.stack(offsets).astype(jnp.int32)
    mixed, qt, ot, lse = attention_forward(bounds, queries, cos_t, sin_t, start_row, blocks, [])
    residual, hidden_two, full_out = output_of(
        offsets_qkv, tokens[0], mixed, gain_two, pieces_out, [later[r] for r in later]
    )

    cot = cotangent[0]
    hiddens = gather_rel(hidden_two, "seq")
    cots = gather_rel(after(cot, hiddens[group // 2]), "seq")
    terms_out, terms_back, products, grads = {}, {}, [], []
    for r in range(0, group, 2):
        got = feed(offsets, [hiddens[r], hiddens[r + 1]], [cots[r], cots[r + 1]], pieces, down)
        products.append(got[0])
        grads.append(got[1])
        terms_out[r], terms_out[r + 1], terms_back[r], terms_back[r + 1] = got[2:]
    hiddens = [hiddens[r] for r in range(group)]
    cots = [cots[r] for r in range(group)]
    total = lax.axis_size("dp")
    depth = total.bit_length() - 1
    levels = group.bit_length() - 1
    line = Line()
    count = inner // FB
    cuts = [0, -(-count // 2), count]
    share = 2 * slice_d // total
    order = jnp.stack(order).astype(jnp.int32)
    which = fast.astype(jnp.int32)[None]

    for b in reversed(bits_down(group)):
        got = {r: swap(terms_back[r ^ b], "seq", b) for r in terms_back if not r & b}
        if b < group // 2:
            terms_back = {
                r: (terms_back[r].astype(F32) + v.astype(F32)).astype(BF16) for r, v in got.items()
            }
    back_mine, back_send, back_got = terms_back[0], terms_back[group // 2], got[0]
    grad_gu = grad_gate_up_of(grads, hiddens, group, total, [])
    half_rows = slice_f // 2
    down_at = shift + half_rows * jnp.stack([fast, 1 - fast])
    down_keep, down_send = grad_down_of(
        products, cots, down_at.astype(jnp.int32), half_rows, [grad_gu, back_send]
    )
    grad_gu = lax.psum_scatter(
        grad_gu.reshape(total * group * share, inner), "dp", scatter_dimension=0, tiled=True
    ).reshape(group, share, inner)
    down_steps = steps_of_sum(line, down_keep, down_send)
    next(down_steps)
    f32 = lambda *shape: jax.ShapeDtypeStruct(shape, F32)
    bf16 = lambda *shape: jax.ShapeDtypeStruct(shape, BF16)

    grad_residual, grad_mixed, grad_gain_two = single_call(
        lambda _, *refs: residual_back_kernel(*refs), "norm_back",
        (back_mine, back_got, cot, residual, gain_two, full_out), [down_keep],
        [f32(rows, width), bf16(rows, width), f32(1, width)],
    )
    line.mark(grad_mixed)
    next(down_steps)
    dq, *dkv = attention_backward(
        bounds, qt, ot, lse, grad_mixed, cos_t, sin_t, start_row, blocks, line.last
    )
    line.mark(dq)
    dkv_steps = steps_of_scatter(dict(enumerate(dkv)), "seq")
    next(dkv_steps)
    for _ in range(levels - 1):
        next(dkv_steps)
    dkv_mine, dkv_got = next(dkv_steps)
    qkv_width = w_qkv.shape[1]
    joint_width = qkv_width + width
    extra = -slice_d % (8 * total) or 8 * total
    joint_rows = slice_d + extra
    weights = [bf16(joint_rows, joint_width)] * group if aligned else [bf16(width, joint_width)]
    grad_inputs, grad_gain_one, grad_bias, *joint = single_call(
        functools.partial(project_back_kernel, aligned), "project_back",
        (tokens[0], gain_one, hidden_one, dq, dkv_mine, dkv_got, full_qkv, grad_residual, mixed, cos_k, sin_k),
        line.last,
        [f32(rows, width), f32(1, width), f32(1, qkv_width), *weights,
         pltpu.VMEM((rows, qkv_width), BF16), pltpu.VMEM((width, joint_width), BF16)],
        order * slice_d,
    )

    rest = jnp.concatenate(
        [
            grad_gain_one.reshape(group, slice_d),
            grad_gain_two.reshape(group, slice_d),
            grad_bias.reshape(group, slice_b),
        ],
        axis=1,
    ).astype(BF16)
    rest = jnp.pad(rest[:, None, :], ((0, 0), (0, 0), (0, joint_width - rest.shape[1])))
    if not aligned:
        joint = [
            jnp.pad(lax.dynamic_slice_in_dim(joint[0], order[r] * slice_d, slice_d, 0), ((0, extra), (0, 0)))
            for r in range(group)
        ]
    joint = {
        r: lax.dynamic_update_slice_in_dim(v, pick(rest, order[r]), slice_d, 0) for r, v in enumerate(joint)
    }
    line.last = [*line.last, grad_inputs]
    line.mark(grad_inputs)
    for b in reversed(bits_down(group)):
        got = {r: swap(joint[r ^ b], "seq", b) for r in joint if not r & b}
        if b == group // 2:
            next(down_steps)
            for _ in range(2 * (depth - 3)):
                next(down_steps)
        joint = {r: line.mark(add(joint[r][None], v, line.last))[0] for r, v in got.items()}
    joint = lax.all_to_all(joint[0], "dp", 0, 0, tiled=True)
    next(down_steps)
    next(down_steps)
    moved = [pick(grad_gu, order[r]) for r in range(group)]
    moved = [swap(v, "seq", r) if r else v for r, v in enumerate(moved)]
    columns = inner // 2
    parts = [
        line.mark(put_ordered([v[:, at : at + columns] for v in moved], order, line.last))
        for at in (0, columns)
    ]
    first_steps = steps_of_gather(line, parts[0], reversed(range(depth)))
    next(first_steps)
    second_steps = steps_of_gather(line, parts[1], [0, *reversed(range(1, depth))])
    next(second_steps)
    next(down_steps)
    out_steps = steps_of_scatter(terms_out, "seq")
    next(out_steps)
    next(second_steps)
    next(first_steps)
    shape = (total, joint_rows // total, joint_width)

    def spread(_, x, out):
        out[...] = jnp.broadcast_to(jnp.sum(x[...].astype(F32), axis=0).astype(BF16)[None], shape)

    (joint,) = single_call(spread, "sum_and_spread", (joint.reshape(shape),), line.last, [bf16(*shape)])
    line.mark(joint)
    joint = lax.all_to_all(joint.reshape(joint_rows, joint_width), "dp", 0, 0, tiled=True)
    for _ in range(levels - 1):
        next(out_steps)
    for _ in range(depth - 3):
        next(first_steps)
        next(second_steps)
    low, high = next(down_steps)
    down_sum = jnp.concatenate([low.reshape(-1, width), high.reshape(-1, width)]).astype(F32)
    next(first_steps)
    next(second_steps)
    out_mine, out_got = next(out_steps)
    layer_out = (residual + out_mine.astype(F32) + out_got.astype(F32)).astype(BF16)
    joint = joint.astype(F32)
    second = jnp.stack(next(second_steps))
    first = next(first_steps)
    second = jnp.moveaxis(second, depth - 1, 0)
    rest = joint[slice_d]
    lows, highs = [], []
    for i, done in enumerate((first, second)):
        for kept, v in zip((lows, highs), done):
            v = jnp.moveaxis(v, depth - 1, 0).reshape(group, slice_d, columns)
            kept.append((i * columns, v))
    gate_sum = join(lows, firsts, hidden_units)
    up_sum = join(highs, firsts, hidden_units)
    return (
        layer_out[None],
        grad_inputs[None],
        rest[:slice_d],
        joint[:slice_d, :qkv_width],
        rest[2 * slice_d : 2 * slice_d + slice_b],
        joint[:slice_d, qkv_width:],
        rest[slice_d : 2 * slice_d],
        gate_sum,
        up_sum,
        down_sum,
    )


def solution(mesh):
    return jax.shard_map(
        per_device,
        mesh=mesh,
        in_specs=(
            P("dp", "seq", None),
            P("dp", None),
            P("dp", "seq", None),
            P("seq"),
            P("seq", None),
            P("seq"),
            P("seq", None),
            P("seq"),
            P("seq", None),
            P("seq", None),
            P("seq", None),
        ),
        out_specs=(
            P("dp", "seq", None),
            P("dp", "seq", None),
            P("seq"),
            P("seq", None),
            P("seq"),
            P("seq", None),
            P("seq"),
            P("seq", None),
            P("seq", None),
            P("seq", None),
        ),
        check_vma=False,
    )
```

```python
import functools

import jax
import jax.numpy as jnp
from jax import lax
from jax.experimental import pallas as pl
from jax.experimental.pallas import tpu as pltpu
from jax.sharding import PartitionSpec as P

HEADS = 14
KV_HEADS = 2
HEAD_DIM = 64
GROUP = HEADS // KV_HEADS
EPSILON = 1e-06
ROPE_BASE = 1000000.0
SCALE = HEAD_DIM ** (-0.5)
QB = 128
KB = 256
BF16 = jnp.bfloat16
F32 = jnp.float32


def dot_rows(left, right):
    return lax.dot_general(left, right, (((0,), (0,)), ((), ())), preferred_element_type=F32)


def dot_last(left, right):
    return lax.dot_general(left, right, (((1,), (1,)), ((), ())), preferred_element_type=F32)


def dot(left, right):
    return jnp.dot(left, right, preferred_element_type=F32)


def swap(x, axis, mask):
    return lax.ppermute(x, axis, [(i, i ^ mask) for i in range(lax.axis_size(axis))])


def after(x, *deps):
    return lax.optimization_barrier((x, *deps))[0]


def pick(x, index):
    return lax.dynamic_index_in_dim(x, index, 0, keepdims=False)


def bits_down(n):
    bits = []
    b = n // 2
    while b:
        bits.append(b)
        b //= 2
    return bits


def gather_rel(x, axis):
    blocks = {0: x}
    for b in bits_down(lax.axis_size(axis)):
        blocks.update({r ^ b: swap(v, axis, b) for r, v in list(blocks.items())})
    return blocks


def scatter_rel(parts, axis):
    parts = dict(parts)
    for b in reversed(bits_down(lax.axis_size(axis))):
        kept = {}
        for r in [r for r in parts if not r & b]:
            kept[r] = (parts[r].astype(F32) + swap(parts[r ^ b], axis, b).astype(F32)).astype(BF16)
        parts = kept
    return parts[0]


def place(blocks, index):
    rows = blocks[0].shape[0]
    out = jnp.zeros((rows * len(blocks),) + blocks[0].shape[1:], blocks[0].dtype)
    for r, v in blocks.items():
        out = lax.dynamic_update_slice_in_dim(out, v, (index ^ r) * rows, 0)
    return out


def masks(start_ref, first_query, first_key):
    key = first_key + lax.broadcasted_iota(jnp.int32, (KB, QB), 0)
    query = first_query + lax.broadcasted_iota(jnp.int32, (KB, QB), 1)
    fine = (key >= start_ref[...]) & (key <= query)
    bias = jnp.where(fine, 0.0, -1e30).astype(F32)
    return jnp.concatenate([bias] * GROUP, axis=1)


def collect(bounds, blocks, k_ref, v_ref):
    me = bounds[bounds.shape[0] - 1]
    for r, block in enumerate(blocks):
        rows = block.shape[0]
        at = pl.multiple_of((me ^ r) * rows, QB)
        k_ref[pl.ds(at, rows), :] = block[:, : 2 * HEAD_DIM]
        v_ref[pl.ds(at, rows), :] = block[:, 2 * HEAD_DIM :]


def turn_over(source, target):
    for at in range(0, source.shape[0], QB):
        target[:, at : at + QB] = source[at : at + QB, :].astype(F32).T.astype(BF16)


def forward_kernel(group, bounds, pq_ref, cos_ref, sin_ref, start_ref, *rest):
    blocks = rest[:group]
    o_ref, qt_ref, ot_ref, lse_ref, qpad, top, total, acc, k_ref, v_ref, vt_ref = rest[-11:]
    b = pl.program_id(0)

    @pl.when(b == 0)
    def _():
        collect(bounds, blocks, k_ref, v_ref)
        turn_over(v_ref, vt_ref)

    lo, hi, first = bounds[3 * b], bounds[3 * b + 1], bounds[3 * b + 2]
    half = HEAD_DIM // 2
    turned = pq_ref[...].T
    cosine, sine = cos_ref[...], sin_ref[...]
    qpad[...] = jnp.zeros_like(qpad)
    for h in range(HEADS):
        g, i = divmod(h, GROUP)
        u1 = turned[h * HEAD_DIM : h * HEAD_DIM + half]
        u2 = turned[h * HEAD_DIM + half : (h + 1) * HEAD_DIM]
        both = jnp.concatenate([u1 * cosine - u2 * sine, u2 * cosine + u1 * sine], axis=0)
        both = both.astype(BF16) * jnp.asarray(SCALE, BF16)
        qpad[g, g * HEAD_DIM : (g + 1) * HEAD_DIM, i * QB : (i + 1) * QB] = both
        qt_ref[0, g, :, i * QB : (i + 1) * QB] = both
    top[...] = jnp.full_like(top, -1e30)
    total[...] = jnp.zeros_like(total)
    acc[...] = jnp.zeros_like(acc)

    def step(j, _):
        at = pl.multiple_of(j * KB, KB)
        keys = k_ref[pl.ds(at, KB), :]
        bias = masks(start_ref, first, at)
        for g in range(KV_HEADS):
            scores = dot(keys, qpad[g]) + bias
            new_top = jnp.maximum(top[g], jnp.max(scores, axis=0, keepdims=True))
            weights = jnp.exp(scores - new_top)
            fade = jnp.exp(top[g] - new_top)
            total[g] = total[g] * fade + jnp.sum(weights, axis=0, keepdims=True)
            values = vt_ref[g * HEAD_DIM : (g + 1) * HEAD_DIM, pl.ds(at, KB)]
            acc[g] = acc[g] * fade + dot(values, weights.astype(BF16))
            top[g] = new_top
        return 0

    lax.fori_loop(lo, hi, step, 0)
    pieces = []
    for g in range(KV_HEADS):
        mixed = acc[g] / total[g]
        ot_ref[0, g] = mixed.astype(BF16)
        lse_ref[0, g] = top[g] + jnp.log(total[g])
        pieces += [mixed[:, i * QB : (i + 1) * QB] for i in range(GROUP)]
    o_ref[...] = jnp.concatenate(pieces, axis=0).T.astype(BF16)


def backward_kernel(
    group, waits, bounds, qt_ref, ot_ref, lse_ref, do_ref, cos_ref, sin_ref, start_ref, *rest
):
    blocks, rest = rest[:group], rest[group + waits :]
    dq_ref, dkv_refs, rest = rest[0], rest[1 : 1 + group], rest[1 + group :]
    qpad, dopad, qrow, dorow, centre, dqt, dk_acc, dv_acc, k_ref, v_ref, kt_ref = rest
    b = pl.program_id(0)
    lo, hi, first = bounds[3 * b], bounds[3 * b + 1], bounds[3 * b + 2]
    half = HEAD_DIM // 2

    @pl.when(b == 0)
    def _():
        dk_acc[...] = jnp.zeros_like(dk_acc)
        dv_acc[...] = jnp.zeros_like(dv_acc)
        collect(bounds, blocks, k_ref, v_ref)
        turn_over(k_ref, kt_ref)

    qpad[...] = jnp.zeros_like(qpad)
    dopad[...] = jnp.zeros_like(dopad)
    dqt[...] = jnp.zeros_like(dqt)
    grads = do_ref[...].astype(F32)
    turned = grads.T
    lane = lax.broadcasted_iota(jnp.int32, (QB, 2 * HEAD_DIM), 1)
    for h in range(HEADS):
        g, i = divmod(h, GROUP)
        rows = slice(g * HEAD_DIM, (g + 1) * HEAD_DIM)
        cols = slice(i * QB, (i + 1) * QB)
        grad_t = turned[h * HEAD_DIM : (h + 1) * HEAD_DIM]
        dopad[g, rows, cols] = grad_t.astype(BF16)
        centre[g, :, cols] = jnp.sum(grad_t * ot_ref[0, g, :, cols].astype(F32), axis=0, keepdims=True)
        query_t = qt_ref[0, g, :, cols]
        qpad[g, rows, cols] = query_t
        mine = (lane >= g * HEAD_DIM) & (lane < (g + 1) * HEAD_DIM)
        pair = grads[:, (h // 2) * 2 * HEAD_DIM : (h // 2 + 1) * 2 * HEAD_DIM]
        if h % 2 != g:
            pair = pltpu.roll(pair, HEAD_DIM, 1)
        dorow[g, cols, :] = jnp.where(mine, pair, 0.0).astype(BF16)
        wide = qpad[g, :, cols].astype(F32)
        qrow[g, cols, :] = wide.T.astype(BF16)

    def step(j, _):
        at = pl.multiple_of(j * KB, KB)
        keys = k_ref[pl.ds(at, KB), :]
        values = v_ref[pl.ds(at, KB), :]
        bias = masks(start_ref, first, at)
        dk_term = None
        dv_term = None
        for g in range(KV_HEADS):
            probs = jnp.exp(dot(keys, qpad[g]) + bias - lse_ref[0, g])
            grad_probs = dot(values, dopad[g])
            grad_scores = (probs * (grad_probs - centre[g])).astype(BF16)
            dv_g = dot(probs.astype(BF16), dorow[g])
            dk_g = dot(grad_scores, qrow[g])
            dk_term = dk_g if g == 0 else dk_term + dk_g
            dv_term = dv_g if g == 0 else dv_term + dv_g
            turned_keys = kt_ref[g * HEAD_DIM : (g + 1) * HEAD_DIM, pl.ds(at, KB)]
            dqt[g] += dot(turned_keys, grad_scores)
        dk_acc[pl.ds(at, KB), :] += dk_term
        dv_acc[pl.ds(at, KB), :] += dv_term
        return 0

    lax.fori_loop(lo, hi, step, 0)
    cosine, sine = cos_ref[...], sin_ref[...]
    pieces = []
    for h in range(HEADS):
        g, i = divmod(h, GROUP)
        w1 = dqt[g, :half, i * QB : (i + 1) * QB] * SCALE
        w2 = dqt[g, half:, i * QB : (i + 1) * QB] * SCALE
        pieces += [w1 * cosine + w2 * sine, w2 * cosine - w1 * sine]
    dq_ref[...] = jnp.concatenate(pieces, axis=0).T.astype(BF16)

    @pl.when(b == pl.num_programs(0) - 1)
    def _():
        me = bounds[bounds.shape[0] - 1]
        for r, ref in enumerate(dkv_refs):
            rows = ref.shape[0]
            at = pl.multiple_of((me ^ r) * rows, QB)
            ref[:, : 2 * HEAD_DIM] = dk_acc[pl.ds(at, rows), :].astype(BF16)
            ref[:, 2 * HEAD_DIM :] = dv_acc[pl.ds(at, rows), :].astype(BF16)


def whole(shape):
    return pl.BlockSpec(shape, lambda b, *_: (0,) * len(shape))


def attention_forward(bounds, pq, cos_t, sin_t, start, blocks, waits):
    rows = pq.shape[0]
    length = rows * len(blocks)
    count = rows // QB
    width = HEADS * HEAD_DIM
    lanes = GROUP * QB
    return pl.pallas_call(
        functools.partial(forward_kernel, len(blocks)),
        out_shape=(
            jax.ShapeDtypeStruct((rows, width), BF16),
            jax.ShapeDtypeStruct((count, KV_HEADS, HEAD_DIM, lanes), BF16),
            jax.ShapeDtypeStruct((count, KV_HEADS, HEAD_DIM, lanes), BF16),
            jax.ShapeDtypeStruct((count, KV_HEADS, 1, lanes), F32),
        ),
        grid_spec=pltpu.PrefetchScalarGridSpec(
            num_scalar_prefetch=1,
            grid=(count,),
            in_specs=[
                pl.BlockSpec((QB, width), lambda b, *_: (b, 0)),
                pl.BlockSpec((HEAD_DIM // 2, QB), lambda b, *_: (0, b)),
                pl.BlockSpec((HEAD_DIM // 2, QB), lambda b, *_: (0, b)),
                pl.BlockSpec((1, QB), lambda b, *_: (0, b)),
                *[whole((rows, 4 * HEAD_DIM))] * len(blocks),
                *[pl.BlockSpec(memory_space=pl.ANY)] * len(waits),
            ],
            out_specs=[
                pl.BlockSpec((QB, width), lambda b, *_: (b, 0)),
                pl.BlockSpec((1, KV_HEADS, HEAD_DIM, lanes), lambda b, *_: (b, 0, 0, 0)),
                pl.BlockSpec((1, KV_HEADS, HEAD_DIM, lanes), lambda b, *_: (b, 0, 0, 0)),
                pl.BlockSpec((1, KV_HEADS, 1, lanes), lambda b, *_: (b, 0, 0, 0)),
            ],
            scratch_shapes=[
                pltpu.VMEM((KV_HEADS, 2 * HEAD_DIM, lanes), BF16),
                pltpu.VMEM((KV_HEADS, 1, lanes), F32),
                pltpu.VMEM((KV_HEADS, 1, lanes), F32),
                pltpu.VMEM((KV_HEADS, HEAD_DIM, lanes), F32),
                pltpu.VMEM((length, 2 * HEAD_DIM), BF16),
                pltpu.VMEM((length, 2 * HEAD_DIM), BF16),
                pltpu.VMEM((2 * HEAD_DIM, length), BF16),
            ],
        ),
        compiler_params=pltpu.CompilerParams(vmem_limit_bytes=40 << 20),
        cost_estimate=pl.CostEstimate(
            flops=1 << 22, bytes_accessed=1 << 18, transcendentals=0
        ),
        name="attention_forward",
    )(bounds, pq, cos_t, sin_t, start, *blocks, *waits)


def attention_backward(bounds, qt, ot, lse, grad_mixed, cos_t, sin_t, start, blocks, waits):
    rows = grad_mixed.shape[0]
    group = len(blocks)
    length = rows * group
    count = rows // QB
    width = HEADS * HEAD_DIM
    lanes = GROUP * QB
    return pl.pallas_call(
        functools.partial(backward_kernel, group, len(waits)),
        out_shape=(
            jax.ShapeDtypeStruct((rows, width), BF16),
            *[jax.ShapeDtypeStruct((rows, 4 * HEAD_DIM), BF16)] * group,
        ),
        grid_spec=pltpu.PrefetchScalarGridSpec(
            num_scalar_prefetch=1,
            grid=(count,),
            in_specs=[
                pl.BlockSpec((1, KV_HEADS, HEAD_DIM, lanes), lambda b, *_: (b, 0, 0, 0)),
                pl.BlockSpec((1, KV_HEADS, HEAD_DIM, lanes), lambda b, *_: (b, 0, 0, 0)),
                pl.BlockSpec((1, KV_HEADS, 1, lanes), lambda b, *_: (b, 0, 0, 0)),
                pl.BlockSpec((QB, width), lambda b, *_: (b, 0)),
                pl.BlockSpec((HEAD_DIM // 2, QB), lambda b, *_: (0, b)),
                pl.BlockSpec((HEAD_DIM // 2, QB), lambda b, *_: (0, b)),
                pl.BlockSpec((1, QB), lambda b, *_: (0, b)),
                *[whole((rows, 4 * HEAD_DIM))] * group,
                *[pl.BlockSpec(memory_space=pl.ANY)] * len(waits),
            ],
            out_specs=[
                pl.BlockSpec((QB, width), lambda b, *_: (b, 0)),
                *[whole((rows, 4 * HEAD_DIM))] * group,
            ],
            scratch_shapes=[
                pltpu.VMEM((KV_HEADS, 2 * HEAD_DIM, lanes), BF16),
                pltpu.VMEM((KV_HEADS, 2 * HEAD_DIM, lanes), BF16),
                pltpu.VMEM((KV_HEADS, lanes, 2 * HEAD_DIM), BF16),
                pltpu.VMEM((KV_HEADS, lanes, 2 * HEAD_DIM), BF16),
                pltpu.VMEM((KV_HEADS, 1, lanes), F32),
                pltpu.VMEM((KV_HEADS, HEAD_DIM, lanes), F32),
                pltpu.VMEM((length, 2 * HEAD_DIM), F32),
                pltpu.VMEM((length, 2 * HEAD_DIM), F32),
                pltpu.VMEM((length, 2 * HEAD_DIM), BF16),
                pltpu.VMEM((length, 2 * HEAD_DIM), BF16),
                pltpu.VMEM((2 * HEAD_DIM, length), BF16),
            ],
        ),
        compiler_params=pltpu.CompilerParams(vmem_limit_bytes=48 << 20),
        cost_estimate=pl.CostEstimate(
            flops=1 << 22, bytes_accessed=1 << 18, transcendentals=0
        ),
        name="attention_backward",
    )(bounds, qt, ot, lse, grad_mixed, cos_t, sin_t, start, *blocks, *waits)


def project_kernel(offsets, x_ref, gain_ref, bias_ref, cos_ref, sin_ref, *rest):
    pieces = rest[:-6]
    pass_ref, q_ref, kv_ref, hidden_ref, w_ref, passed_ref = rest[-6:]
    passed_ref[...] = pass_ref[...]
    for i, piece in enumerate(pieces):
        count = piece.shape[0]
        w_ref[pl.ds(pl.multiple_of(offsets[i], 16), count), :] = piece[...]
    x = x_ref[...].astype(F32)
    scale = lax.rsqrt(jnp.mean(x * x, axis=-1, keepdims=True) + EPSILON)
    hidden = (x * scale * gain_ref[...]).astype(BF16)
    hidden_ref[...] = hidden
    query_width = HEADS * HEAD_DIM
    key_width = KV_HEADS * HEAD_DIM
    q_ref[...] = dot(hidden, w_ref[:, :query_width]) + bias_ref[:, :query_width]
    kv = dot(hidden, w_ref[:, query_width:]) + bias_ref[:, query_width:]
    keys = kv[:, :key_width]
    lane = lax.broadcasted_iota(jnp.int32, keys.shape, 1) % HEAD_DIM
    half = HEAD_DIM // 2
    other = jnp.where(
        lane < half, pltpu.roll(keys, key_width - half, 1), pltpu.roll(keys, half, 1)
    )
    keys = keys * cos_ref[...] + other * sin_ref[...]
    kv_ref[:, :key_width] = keys.astype(BF16)
    kv_ref[:, key_width:] = kv[:, key_width:].astype(BF16)


def project(offsets, x, gain, bias, cosine, sine, pieces, passed):
    rows, width = x.shape
    total = bias.shape[1]
    query_width = HEADS * HEAD_DIM
    return pl.pallas_call(
        project_kernel,
        out_shape=(
            jax.ShapeDtypeStruct((rows, query_width), F32),
            jax.ShapeDtypeStruct((rows, total - query_width), BF16),
            jax.ShapeDtypeStruct((rows, width), BF16),
            jax.ShapeDtypeStruct((width, total), BF16),
            jax.ShapeDtypeStruct(passed.shape, BF16),
        ),
        grid_spec=pltpu.PrefetchScalarGridSpec(
            num_scalar_prefetch=1,
            grid=(1,),
            in_specs=[whole(v.shape) for v in (x, gain, bias, cosine, sine, *pieces, passed)],
            out_specs=[
                whole((rows, query_width)),
                whole((rows, total - query_width)),
                whole((rows, width)),
                whole((width, total)),
                whole(passed.shape),
            ],
        ),
        compiler_params=pltpu.CompilerParams(vmem_limit_bytes=40 << 20),
        cost_estimate=pl.CostEstimate(
            flops=2 * rows * width * total, bytes_accessed=8 << 20, transcendentals=0
        ),
        name="norm_project_rotate",
    )(offsets, x, gain, bias, cosine, sine, *pieces, passed)


def output_kernel(pieces, offsets, x_ref, mixed_ref, gain_ref, *rest):
    residual_ref, hidden_ref, w_ref = rest[-3:]
    for i, piece in enumerate(rest[:pieces]):
        w_ref[pl.ds(pl.multiple_of(offsets[i], 16), piece.shape[0]), :] = piece[...]
    residual = x_ref[...].astype(F32) + dot(mixed_ref[...], w_ref[...])
    residual_ref[...] = residual
    scale = lax.rsqrt(jnp.mean(residual * residual, axis=-1, keepdims=True) + EPSILON)
    hidden_ref[...] = (residual * scale * gain_ref[...]).astype(BF16)


def output_of(offsets, x, mixed, gain, pieces, waits):
    rows, width = x.shape
    return pl.pallas_call(
        functools.partial(output_kernel, len(pieces)),
        out_shape=(
            jax.ShapeDtypeStruct((rows, width), F32),
            jax.ShapeDtypeStruct((rows, width), BF16),
            jax.ShapeDtypeStruct((width, width), BF16),
        ),
        grid_spec=pltpu.PrefetchScalarGridSpec(
            num_scalar_prefetch=1,
            grid=(1,),
            in_specs=[
                *[whole(v.shape) for v in (x, mixed, gain, *pieces)],
                *[pl.BlockSpec(memory_space=pl.ANY)] * len(waits),
            ],
            out_specs=[whole((rows, width)), whole((rows, width)), whole((width, width))],
        ),
        compiler_params=pltpu.CompilerParams(vmem_limit_bytes=40 << 20),
        cost_estimate=pl.CostEstimate(flops=1 << 22, bytes_accessed=1 << 18, transcendentals=0),
        name="project_add_norm",
    )(offsets, x, mixed, gain, *pieces, *waits)


FB = 256


def feed_kernel(blocks, offsets, *refs):
    hs, dys, refs = refs[:blocks], refs[blocks : 2 * blocks], refs[2 * blocks :]
    count = offsets.shape[0]
    pieces, refs = refs[:count], refs[count:]
    wd_ref, m_ref, d_ref = refs[:3]
    outs, backs = refs[3 : 3 + blocks], refs[3 + blocks : 3 + 2 * blocks]
    out_acc, dh_acc, wg, wu = refs[3 + 2 * blocks :]
    step = pl.program_id(0)
    last = pl.num_programs(0) - 1
    rows = hs[0].shape[0]
    for i, piece in enumerate(pieces):
        at = pl.ds(pl.multiple_of(offsets[i], 16), piece.shape[1])
        wg[at, :] = piece[0]
        wu[at, :] = piece[1]

    @pl.when(step == 0)
    def _():
        out_acc[...] = jnp.zeros_like(out_acc)
        dh_acc[...] = jnp.zeros_like(dh_acc)

    for t in range(blocks):
        at = slice(t * rows, (t + 1) * rows)
        hidden, cot = hs[t][...], dys[t][...]
        gate = dot(hidden, wg[...])
        upward = dot(hidden, wu[...])
        grad_product = dot_last(cot, wd_ref[...])
        sigma = jax.nn.sigmoid(gate)
        active = gate * sigma
        product = (active * upward).astype(BF16)
        grad_gate = (grad_product * upward * (sigma + active * (1.0 - sigma))).astype(BF16)
        grad_up = (grad_product * active).astype(BF16)
        d_ref[0, at], d_ref[1, at] = grad_gate, grad_up
        m_ref[:, at] = (active * upward).T.astype(BF16)
        out_acc[at] += dot(product, wd_ref[...])
        dh_acc[at] += dot_last(grad_gate, wg[...]) + dot_last(grad_up, wu[...])

    @pl.when(step == last)
    def _():
        for t in range(blocks):
            at = slice(t * rows, (t + 1) * rows)
            outs[t][...] = out_acc[at].astype(BF16)
            backs[t][...] = dh_acc[at].astype(BF16)


def feed(offsets, hiddens, cots, pieces, w_down):
    blocks = len(hiddens)
    rows, width = hiddens[0].shape
    inner = w_down.shape[0]
    wide = jax.ShapeDtypeStruct((2, blocks * rows, inner), BF16)
    tall = jax.ShapeDtypeStruct((inner, blocks * rows), BF16)
    narrow = jax.ShapeDtypeStruct((rows, width), BF16)
    return pl.pallas_call(
        functools.partial(feed_kernel, blocks),
        out_shape=(tall, wide) + (narrow,) * (2 * blocks),
        grid_spec=pltpu.PrefetchScalarGridSpec(
            num_scalar_prefetch=1,
            grid=(inner // FB,),
            in_specs=[
                *[whole((rows, width))] * (2 * blocks),
                *[pl.BlockSpec((2, v.shape[1], FB), lambda j, *_: (0, 0, j)) for v in pieces],
                pl.BlockSpec((FB, width), lambda j, *_: (j, 0)),
            ],
            out_specs=[
                pl.BlockSpec((FB, blocks * rows), lambda j, *_: (j, 0)),
                pl.BlockSpec((2, blocks * rows, FB), lambda j, *_: (0, 0, j)),
                *[whole((rows, width))] * (2 * blocks),
            ],
            scratch_shapes=[
                pltpu.VMEM((blocks * rows, width), F32),
                pltpu.VMEM((blocks * rows, width), F32),
                pltpu.VMEM((width, FB), BF16),
                pltpu.VMEM((width, FB), BF16),
            ],
        ),
        compiler_params=pltpu.CompilerParams(vmem_limit_bytes=48 << 20),
        cost_estimate=pl.CostEstimate(
            flops=1 << 22, bytes_accessed=1 << 18, transcendentals=0
        ),
        name="feed_forward_backward",
    )(offsets, *hiddens, *cots, *pieces, w_down)


def down_kernel(parts, per, cut, offsets, *refs):
    ms, dys, outs = refs[:parts], refs[parts : parts + parts * per], refs[-2:]
    for k, out_ref in enumerate(outs):
        rows = out_ref.shape[0]

        @pl.when(pl.program_id(0) == 1 - k)
        def _():
            total = None
            for i, m_ref in enumerate(ms):
                width = m_ref.shape[-1] // per
                for t in range(per):
                    if cut:
                        at = pl.ds(pl.multiple_of(offsets[k], 16), rows)
                        left = m_ref[at, t * width : (t + 1) * width]
                    else:
                        left = m_ref[k, :, t * width : (t + 1) * width]
                    term = dot(left, dys[i * per + t][...])
                    total = term if total is None else total + term
            out_ref[...] = total.astype(BF16)


def grad_down_of(products, cots, offsets, half, waits):
    rows, width = cots[0].shape
    cut = half % 16 == 0
    if not cut:
        products = [
            jnp.stack([lax.dynamic_slice_in_dim(v, offsets[k], half, 0) for k in range(2)]) for v in products
        ]
    out = jax.ShapeDtypeStruct((half, width), BF16)
    return pl.pallas_call(
        functools.partial(down_kernel, len(products), len(cots) // len(products), cut),
        out_shape=(out, out),
        grid_spec=pltpu.PrefetchScalarGridSpec(
            num_scalar_prefetch=1,
            grid=(2,),
            in_specs=[*[whole(v.shape) for v in (*products, *cots)], *[ANY] * len(waits)],
            out_specs=[whole((half, width))] * 2,
        ),
        compiler_params=pltpu.CompilerParams(vmem_limit_bytes=56 << 20),
        cost_estimate=pl.CostEstimate(flops=1 << 22, bytes_accessed=1 << 18, transcendentals=0),
        name="grad_down",
    )(offsets, *products, *cots, *waits)


def gate_up_kernel(parts, blocks, total, *refs):
    grads, hs, (out, turned) = refs[:parts], refs[parts : parts + blocks], refs[-2:]
    groups, share = out.shape[1:3]
    each = turned.shape[0] // groups

    @pl.when(pl.program_id(0) == 0)
    def _():
        rows = hs[0].shape[0]
        for t, h in enumerate(hs):
            for at in range(0, rows, QB):
                place_at = slice(t * rows + at, t * rows + at + QB)
                turned[:, place_at] = h[at : at + QB, :].astype(F32).T.astype(BF16)

    for i in range(2):
        result = None
        first = 0
        for v in grads:
            term = dot(turned[:, first : first + v.shape[1]], v[i])
            result = term if result is None else result + term
            first += v.shape[1]
        for k in range(total // 2):
            for j in range(groups):
                at = j * each + turned_bits(k, total // 2) * share
                out[2 * k + i, j] = result[at : at + share].astype(BF16)


def turned_bits(k, count):
    out = 0
    while count > 1:
        out, k, count = out * 2 + k % 2, k // 2, count // 2
    return out


def grad_gate_up_of(grads, hiddens, groups, total, waits):
    width = hiddens[0].shape[1]
    tokens = sum(v.shape[1] for v in grads)
    inner = grads[0].shape[2]
    share = 2 * width // (groups * total)
    return pl.pallas_call(
        functools.partial(gate_up_kernel, len(grads), len(hiddens), total),
        out_shape=jax.ShapeDtypeStruct((total, groups, share, inner), BF16),
        grid=(inner // FB,),
        in_specs=[
            *[pl.BlockSpec((2, v.shape[1], FB), lambda j: (0, 0, j)) for v in grads],
            *[whole(v.shape) for v in hiddens],
            *[ANY] * len(waits),
        ],
        out_specs=pl.BlockSpec((total, groups, share, FB), lambda j: (0, 0, 0, j)),
        scratch_shapes=[pltpu.VMEM((width, tokens), BF16)],
        compiler_params=pltpu.CompilerParams(vmem_limit_bytes=56 << 20),
        cost_estimate=pl.CostEstimate(flops=1 << 22, bytes_accessed=1 << 18, transcendentals=0),
        name="grad_gate_up",
    )(*grads, *hiddens, *waits)


def residual_back_kernel(mine_ref, got_ref, cot_ref, residual_ref, gain_ref, w_ref, *rest):
    grad_ref, mixed_ref, gain_out = rest[-3:]
    grad_hidden = mine_ref[...].astype(F32) + got_ref[...].astype(F32)
    residual = residual_ref[...]
    scale = lax.rsqrt(jnp.mean(residual * residual, axis=-1, keepdims=True) + EPSILON)
    normed = residual * scale
    gain_out[...] = jnp.sum(grad_hidden * normed, axis=0, keepdims=True)
    grad = cot_ref[...].astype(F32) + norm_back(grad_hidden, normed, scale, gain_ref[...])
    grad_ref[...] = grad
    mixed_ref[...] = dot_last(grad.astype(BF16), w_ref[...]).astype(BF16)


def single_call(kernel, name, ins, waits, outs, scalars=None):
    scalars = jnp.zeros((1,), jnp.int32) if scalars is None else scalars
    scratch = [v for v in outs if isinstance(v, type(pltpu.VMEM((8, 128), F32)))]
    outs = [v for v in outs if v not in scratch]

    def body(scalar_ref, *refs):
        kernel(scalar_ref, *refs[: len(ins)], *refs[len(ins) + len(waits) :])

    return pl.pallas_call(
        body,
        out_shape=outs,
        grid_spec=pltpu.PrefetchScalarGridSpec(
            num_scalar_prefetch=1,
            grid=(1,),
            in_specs=[*[whole(v.shape) for v in ins], *[ANY] * len(waits)],
            out_specs=[whole(v.shape) for v in outs],
            scratch_shapes=scratch,
        ),
        compiler_params=pltpu.CompilerParams(vmem_limit_bytes=52 << 20),
        cost_estimate=pl.CostEstimate(flops=1 << 22, bytes_accessed=1 << 18, transcendentals=0),
        name=name,
    )(scalars, *ins, *waits)


def project_back_kernel(
    aligned, offsets, x_ref, gain_ref, hidden_ref, dq_ref, mine_ref, got_ref, w_ref, grad_ref, mixed_ref,
    cos_ref, sin_ref, out_ref, gain_out, bias_out, *rest
):
    weights, (dp_ref, dw_ref) = rest[:-2], rest[-2:]
    query_width = HEADS * HEAD_DIM
    key_width = KV_HEADS * HEAD_DIM
    half = HEAD_DIM // 2
    total = w_ref.shape[1]
    dkv = mine_ref[...].astype(F32) + got_ref[...].astype(F32)
    keys = dkv[:, :key_width]
    lane = lax.broadcasted_iota(jnp.int32, keys.shape, 1) % HEAD_DIM
    other = jnp.where(
        lane < half, pltpu.roll(keys, key_width - half, 1), pltpu.roll(keys, half, 1)
    )
    dp_ref[:, :query_width] = dq_ref[...]
    dp_ref[:, query_width : query_width + key_width] = (
        keys * cos_ref[...] - other * sin_ref[...]
    ).astype(BF16)
    dp_ref[:, query_width + key_width :] = dkv[:, key_width:].astype(BF16)
    grads = dp_ref[...]
    bias_out[...] = jnp.sum(grads.astype(F32), axis=0, keepdims=True)
    back = dot_last(grads, w_ref[...])
    x = x_ref[...].astype(F32)
    scale = lax.rsqrt(jnp.mean(x * x, axis=-1, keepdims=True) + EPSILON)
    normed = x * scale
    gain_out[...] = jnp.sum(back * normed, axis=0, keepdims=True)
    out_ref[...] = grad_ref[...] + norm_back(back, normed, scale, gain_ref[...])
    dw_ref[:, :total] = dot(hidden_ref[...].astype(F32).T.astype(BF16), grads).astype(BF16)
    dw_ref[:, total:] = dot(
        mixed_ref[...].astype(F32).T.astype(BF16), grad_ref[...].astype(BF16)
    ).astype(BF16)
    if aligned:
        rows = dw_ref.shape[0] // len(weights)
        for k, ref in enumerate(weights):
            ref[:rows] = dw_ref[pl.ds(pl.multiple_of(offsets[k], 16), rows), :]
            ref[rows:] = jnp.zeros((ref.shape[0] - rows, ref.shape[1]), BF16)
    else:
        weights[0][...] = dw_ref[...]


ANY = pl.BlockSpec(memory_space=pl.ANY)


class Line:
    def __init__(self):
        self.last = []

    def mark(self, x):
        self.last = [x]
        return x


def small_call(kernel, name, scalars, grid, ins, in_specs, out_shape, out_specs, waits):
    count = len(ins)

    def body(scalar_ref, *refs):
        kernel(scalar_ref, refs[:count], refs[count + len(waits) :])

    return pl.pallas_call(
        body,
        out_shape=out_shape,
        grid_spec=pltpu.PrefetchScalarGridSpec(
            num_scalar_prefetch=1,
            grid=grid,
            in_specs=[*in_specs, *[ANY] * len(waits)],
            out_specs=out_specs,
        ),
        compiler_params=pltpu.CompilerParams(vmem_limit_bytes=40 << 20),
        cost_estimate=pl.CostEstimate(flops=1 << 20, bytes_accessed=1 << 18, transcendentals=0),
        name=name,
    )(scalars, *ins, *waits)


def add_split(x, got, lead, mine, waits):
    columns = x.shape[-1]
    x, got = x.reshape(lead, 2, -1, columns), got.reshape(lead, 2, -1, columns)
    rows = x.shape[2]

    def kernel(_, ins, outs):
        for k in range(2):
            total = ins[2 * k][0, 0].astype(F32) + ins[2 * k + 1][0, 0].astype(F32)
            outs[k][0] = total.astype(BF16)

    keep = pl.BlockSpec((1, 1, rows, columns), lambda i, at: (i, at[0], 0, 0))
    send = pl.BlockSpec((1, 1, rows, columns), lambda i, at: (i, 1 - at[0], 0, 0))
    half = jax.ShapeDtypeStruct((lead, rows, columns), BF16)
    out = pl.BlockSpec((1, rows, columns), lambda i, at: (i, 0, 0))
    return small_call(
        kernel, "add_and_split", mine[None], (lead,), (x, got, x, got), (keep, keep, send, send),
        (half, half), (out, out), waits,
    )


def add_ordered(x, got, order, waits):
    shape = (1,) + x.shape[1:]
    got = got.reshape(x.shape)

    def kernel(_, ins, outs):
        for k, out in enumerate(outs):
            out[...] = (ins[2 * k][...].astype(F32) + ins[2 * k + 1][...].astype(F32)).astype(BF16)

    specs = []
    for k in range(order.shape[0]):
        specs += [pl.BlockSpec(shape, lambda i, at, k=k: (at[k], 0, 0))] * 2
    count = order.shape[0]
    return small_call(
        kernel, "add", order, (1,), (x, got) * count, specs,
        (jax.ShapeDtypeStruct(shape, BF16),) * count, (whole(shape),) * count, waits,
    )


def put_ordered(parts, order, waits, dtype=BF16):
    shape = parts[0].shape
    block = shape[-2:]
    lead = parts[0].size // (block[0] * block[1])
    parts = [v.reshape((lead,) + block) for v in parts]
    count = len(parts)

    def kernel(at, ins, outs):
        for k in range(count):
            outs[0][at[k]] = ins[k][...].astype(dtype)

    (out,) = small_call(
        kernel, "place", order, (lead,), parts,
        [pl.BlockSpec((1,) + block, lambda i, at: (i, 0, 0))] * count,
        (jax.ShapeDtypeStruct((count, lead) + block, dtype),),
        (pl.BlockSpec((count, 1) + block, lambda i, at: (0, i, 0, 0)),), waits,
    )
    return out.reshape((count,) + shape)


def steps_of_sum(line, keep, send):
    index = lax.axis_index("dp")
    depth = lax.axis_size("dp").bit_length() - 1
    bits = [((index >> k) & 1).astype(jnp.int32) for k in range(depth)]
    columns = keep.shape[-1]
    for k in range(depth - 1):
        got = swap(send, "dp", 1 << k)
        yield None
        keep, send = add_split(keep, got, 1, bits[k + 1], line.last)
        line.mark(keep)
    got = swap(send, "dp", 1 << (depth - 1))
    yield None
    part = line.mark(add(keep.reshape(1, -1, columns), got, line.last))
    yield from steps_of_gather(line, part, reversed(range(depth)))


def steps_of_gather(line, part, order):
    index = lax.axis_index("dp")
    order = list(order)
    for k in order:
        bit = ((index >> k) & 1).astype(jnp.int32)
        got = swap(part, "dp", 1 << k)
        yield None
        if k == order[-1]:
            yield jnp.where(bit == 0, part, got), jnp.where(bit == 0, got, part)
        part = line.mark(put_ordered([part, got], jnp.stack([bit, 1 - bit]), line.last))


def add(x, got, waits):
    return add_ordered(x, got, jnp.zeros((1,), jnp.int32), waits)[0]


def steps_of_scatter(parts, axis):
    parts = dict(parts)
    for b in reversed(bits_down(lax.axis_size(axis))):
        got = {r: swap(parts[r ^ b], axis, b) for r in parts if not r & b}
        yield None
        if len(got) == 1:
            yield parts[0], got[0]
        parts = {r: (parts[r].astype(F32) + v.astype(F32)).astype(BF16) for r, v in got.items()}


def pad_rows(x, multiple):
    extra = -x.shape[0] % multiple
    return jnp.pad(x, ((0, extra), (0, 0))) if extra else x


def locate(lengths, where_at):
    starts = jnp.cumsum(lengths) - lengths
    inside = where_at[:, None] >= starts[None, :]
    return jnp.max(jnp.where(inside, starts[None, :], 0), axis=1)


def norm_back(grad_hidden, normed, scale_rows, gain):
    scaled = grad_hidden * gain
    return scale_rows * (scaled - normed * jnp.mean(scaled * normed, axis=-1, keepdims=True))


def turn_heads(values, cosine, sine):
    rows = values.shape[0]
    values = values.reshape(rows, KV_HEADS, HEAD_DIM)
    half = HEAD_DIM // 2
    first, second = values[..., :half], values[..., half:]
    cosine, sine = cosine[:, None, :], sine[:, None, :]
    turned = jnp.concatenate([first * cosine - second * sine, second * cosine + first * sine], axis=-1)
    return turned.reshape(rows, KV_HEADS * HEAD_DIM)


def swaps(x, axis):
    return {r: swap(x, axis, r) if r else x for r in range(lax.axis_size(axis))}


def windows(total, count, tile=128):
    each = total // count
    firsts = [j * each // tile * tile for j in range(count)]
    width = max(j * each - first + each for j, first in enumerate(firsts))
    return -(-width // FB) * FB, firsts


def join(parts, firsts, total, tile=128):
    runs = []
    for at in range(0, total, tile):
        cover = []
        for i, (first, values) in enumerate(parts):
            for j, begin in enumerate(firsts):
                local = at - begin - first
                if 0 <= local < values.shape[-1]:
                    cover.append((i, j, local))
        if runs and [(i, j, c - runs[-1][1]) for i, j, c in cover] == runs[-1][0]:
            runs[-1][1] += tile
        else:
            runs.append([cover, tile])
    segments = []
    for cover, width in runs:
        segments.append(
            sum(parts[i][1][j, :, c : c + width].astype(F32) for i, j, c in cover)
        )
    return jnp.concatenate(segments, axis=1)


def per_device(
    tokens, doc_lengths, cotangent, norm_one, w_qkv, b_qkv, w_out, norm_two, w_gate, w_up, w_down
):
    group = lax.axis_size("seq")
    me = lax.axis_index("seq")
    inputs = tokens[0].astype(F32)
    rows, width = inputs.shape
    query_width = HEADS * HEAD_DIM
    key_width = KV_HEADS * HEAD_DIM
    slice_d = width // group
    slice_b = b_qkv.shape[0]
    slice_f = w_down.shape[0]
    hidden_units = slice_f * group
    aligned = slice_d % 32 == 0

    small = jnp.concatenate([norm_one, norm_two, b_qkv])[None, :]
    small = place(swaps(small, "seq"), me)
    gain_one = small[:, :slice_d].reshape(1, width).astype(F32)
    gain_two = small[:, slice_d : 2 * slice_d].reshape(1, width).astype(F32)
    bias = small[:, 2 * slice_d :].reshape(1, -1).astype(F32)
    pieces_qkv = gather_rel(w_qkv, "seq")
    order = [me ^ r for r in range(group)]
    if aligned:
        offsets_qkv = jnp.stack([j * slice_d for j in order]).astype(jnp.int32)
        pieces_qkv = [pieces_qkv[r] for r in range(group)]
    else:
        offsets_qkv = jnp.zeros((1,), jnp.int32)
        pieces_qkv = [place(pieces_qkv, me)]

    inner, firsts = windows(hidden_units, group)
    both = jnp.stack([w_gate, w_up])
    both = jnp.pad(both, ((0, 0), (0, 0), (0, max(0, firsts[-1] + inner - hidden_units))))
    both = jnp.stack([both[:, :, at : at + inner] for at in firsts])
    shift = lax.rem(me * slice_f, 128)
    down = lax.dynamic_update_slice_in_dim(jnp.zeros((inner, width), BF16), w_down, shift, 0)

    half_d = slice_d // 2
    fast = (lax.axis_index("dp") & 1).astype(jnp.int32)
    slow = ((lax.axis_index("dp") >> 1) & 1).astype(jnp.int32)
    early = {}
    for r in range(2, group):
        part = lax.dynamic_slice(
            both, (order[r], slow, fast * half_d, 0), (1, 1, half_d, inner)
        )
        early[r] = swap(part.reshape(half_d, inner), "seq", r)

    offset = me * rows
    index = offset + jnp.arange(rows, dtype=jnp.int32)
    start = locate(doc_lengths[0], index)
    places = (index - start).astype(F32)
    half = HEAD_DIM // 2
    freqs = ROPE_BASE ** (-(jnp.arange(half, dtype=F32) * 2.0) / HEAD_DIM)
    angle = places[:, None] * freqs[None, :]
    cosine, sine = jnp.cos(angle), jnp.sin(angle)
    cos_t, sin_t = cosine.T, sine.T
    cos_k = jnp.concatenate([cosine] * (2 * KV_HEADS), axis=1)
    sin_k = jnp.concatenate([-sine, sine] * KV_HEADS, axis=1)
    marks = offset + jnp.arange(rows // QB, dtype=jnp.int32) * QB
    bounds = jnp.stack([start[::QB] // KB, (marks + QB - 1) // KB + 1, marks], axis=1).reshape(-1)
    bounds = jnp.concatenate([bounds, me[None]]).astype(jnp.int32)
    start_row = start.astype(jnp.int32)[None, :]

    queries, kv, hidden_one, full_qkv, w_out = project(
        offsets_qkv, tokens[0], gain_one, bias, cos_k, sin_k, pieces_qkv, w_out
    )
    pieces_out = gather_rel(w_out, "seq")
    pieces_out = [pieces_out[r] for r in range(group)] if aligned else [place(pieces_out, me)]
    (kv,) = single_call(
        lambda _, a, b: b.__setitem__(..., a[...]), "pass_on", (kv,), [early[r] for r in early],
        [jax.ShapeDtypeStruct(kv.shape, BF16)],
    )
    blocks = gather_rel(kv, "seq")
    blocks = [blocks[r] for r in range(group)]
    later = {}
    pieces = [pick(both, order[0]), swap(pick(both, order[1]), "seq", 1)]
    offsets = [order[0] * slice_d, order[1] * slice_d]
    for r in range(2, group):
        got = swap(early[r], "dp", 2)
        later[r] = part = put_ordered([early[r], got], jnp.stack([slow, 1 - slow]), [])
        pieces += [part, swap(part, "dp", 1)]
        at = order[r] * slice_d
        offsets += [at + fast * half_d, at + (1 - fast) * half_d]
    if not aligned:
        full = jnp.zeros((2, width, inner), BF16)
        for piece, at in zip(pieces, offsets):
            full = lax.dynamic_update_slice(full, piece, (0, at, 0))
        pieces, offsets = [full], [0 * me]
    offsets = jnp.stack(offsets).astype(jnp.int32)
    mixed, qt, ot, lse = attention_forward(bounds, queries, cos_t, sin_t, start_row, blocks, [])
    residual, hidden_two, full_out = output_of(
        offsets_qkv, tokens[0], mixed, gain_two, pieces_out, [later[r] for r in later]
    )

    cot = cotangent[0]
    hiddens = gather_rel(hidden_two, "seq")
    cots = gather_rel(after(cot, hiddens[group // 2]), "seq")
    terms_out, terms_back, products, grads = {}, {}, [], []
    for r in range(0, group, 2):
        got = feed(offsets, [hiddens[r], hiddens[r + 1]], [cots[r], cots[r + 1]], pieces, down)
        products.append(got[0])
        grads.append(got[1])
        terms_out[r], terms_out[r + 1], terms_back[r], terms_back[r + 1] = got[2:]
    hiddens = [hiddens[r] for r in range(group)]
    cots = [cots[r] for r in range(group)]
    total = lax.axis_size("dp")
    depth = total.bit_length() - 1
    levels = group.bit_length() - 1
    line = Line()
    count = inner // FB
    cuts = [0, -(-count // 2), count]
    share = 2 * slice_d // total
    order = jnp.stack(order).astype(jnp.int32)
    which = fast.astype(jnp.int32)[None]

    for b in reversed(bits_down(group)):
        got = {r: swap(terms_back[r ^ b], "seq", b) for r in terms_back if not r & b}
        if b < group // 2:
            terms_back = {
                r: (terms_back[r].astype(F32) + v.astype(F32)).astype(BF16) for r, v in got.items()
            }
    back_mine, back_send, back_got = terms_back[0], terms_back[group // 2], got[0]
    grad_gu = grad_gate_up_of(grads, hiddens, group, total, [])
    half_rows = slice_f // 2
    down_at = shift + half_rows * jnp.stack([fast, 1 - fast])
    down_keep, down_send = grad_down_of(
        products, cots, down_at.astype(jnp.int32), half_rows, [grad_gu, back_send]
    )
    grad_gu = lax.psum_scatter(
        grad_gu.reshape(total * group * share, inner), "dp", scatter_dimension=0, tiled=True
    ).reshape(group, share, inner)
    down_steps = steps_of_sum(line, down_keep, down_send)
    next(down_steps)
    f32 = lambda *shape: jax.ShapeDtypeStruct(shape, F32)
    bf16 = lambda *shape: jax.ShapeDtypeStruct(shape, BF16)

    grad_residual, grad_mixed, grad_gain_two = single_call(
        lambda _, *refs: residual_back_kernel(*refs), "norm_back",
        (back_mine, back_got, cot, residual, gain_two, full_out), [down_keep],
        [f32(rows, width), bf16(rows, width), f32(1, width)],
    )
    line.mark(grad_mixed)
    dq, *dkv = attention_backward(
        bounds, qt, ot, lse, grad_mixed, cos_t, sin_t, start_row, blocks, line.last
    )
    line.mark(dq)
    next(down_steps)
    dkv_steps = steps_of_scatter(dict(enumerate(dkv)), "seq")
    next(dkv_steps)
    for _ in range(levels - 1):
        next(dkv_steps)
    dkv_mine, dkv_got = next(dkv_steps)
    qkv_width = w_qkv.shape[1]
    joint_width = qkv_width + width
    extra = -slice_d % (8 * total) or 8 * total
    joint_rows = slice_d + extra
    weights = [bf16(joint_rows, joint_width)] * group if aligned else [bf16(width, joint_width)]
    grad_inputs, grad_gain_one, grad_bias, *joint = single_call(
        functools.partial(project_back_kernel, aligned), "project_back",
        (tokens[0], gain_one, hidden_one, dq, dkv_mine, dkv_got, full_qkv, grad_residual, mixed, cos_k, sin_k),
        line.last,
        [f32(rows, width), f32(1, width), f32(1, qkv_width), *weights,
         pltpu.VMEM((rows, qkv_width), BF16), pltpu.VMEM((width, joint_width), BF16)],
        order * slice_d,
    )

    rest = jnp.concatenate(
        [
            grad_gain_one.reshape(group, slice_d),
            grad_gain_two.reshape(group, slice_d),
            grad_bias.reshape(group, slice_b),
        ],
        axis=1,
    ).astype(BF16)
    rest = jnp.pad(rest[:, None, :], ((0, 0), (0, 0), (0, joint_width - rest.shape[1])))
    if not aligned:
        joint = [
            jnp.pad(lax.dynamic_slice_in_dim(joint[0], order[r] * slice_d, slice_d, 0), ((0, extra), (0, 0)))
            for r in range(group)
        ]
    joint = {
        r: lax.dynamic_update_slice_in_dim(v, pick(rest, order[r]), slice_d, 0) for r, v in enumerate(joint)
    }
    line.last = [*line.last, grad_inputs]
    line.mark(grad_inputs)
    for b in reversed(bits_down(group)):
        got = {r: swap(joint[r ^ b], "seq", b) for r in joint if not r & b}
        if b == group // 2:
            next(down_steps)
            for _ in range(2 * (depth - 3)):
                next(down_steps)
        joint = {r: line.mark(add(joint[r][None], v, line.last))[0] for r, v in got.items()}
    joint = lax.all_to_all(joint[0], "dp", 0, 0, tiled=True)
    moved = [pick(grad_gu, order[r]) for r in range(group)]
    moved = [swap(v, "seq", r) if r else v for r, v in enumerate(moved)]
    columns = inner // 2
    parts = [
        line.mark(put_ordered([v[:, at : at + columns] for v in moved], order, line.last))
        for at in (0, columns)
    ]
    first_steps = steps_of_gather(line, parts[0], reversed(range(depth)))
    next(first_steps)
    second_steps = steps_of_gather(line, parts[1], [0, *reversed(range(1, depth))])
    next(second_steps)
    next(down_steps)
    out_steps = steps_of_scatter(terms_out, "seq")
    next(out_steps)
    next(second_steps)
    next(first_steps)
    next(down_steps)
    next(down_steps)
    shape = (total, joint_rows // total, joint_width)

    def spread(_, x, out):
        out[...] = jnp.broadcast_to(jnp.sum(x[...].astype(F32), axis=0).astype(BF16)[None], shape)

    (joint,) = single_call(spread, "sum_and_spread", (joint.reshape(shape),), line.last, [bf16(*shape)])
    line.mark(joint)
    joint = lax.all_to_all(joint.reshape(joint_rows, joint_width), "dp", 0, 0, tiled=True)
    for _ in range(levels - 1):
        next(out_steps)
    for _ in range(depth - 3):
        next(first_steps)
        next(second_steps)
    low, high = next(down_steps)
    down_sum = jnp.concatenate([low.reshape(-1, width), high.reshape(-1, width)]).astype(F32)
    next(first_steps)
    next(second_steps)
    out_mine, out_got = next(out_steps)
    layer_out = (residual + out_mine.astype(F32) + out_got.astype(F32)).astype(BF16)
    joint = joint.astype(F32)
    second = jnp.stack(next(second_steps))
    first = next(first_steps)
    second = jnp.moveaxis(second, depth - 1, 0)
    rest = joint[slice_d]
    lows, highs = [], []
    for i, done in enumerate((first, second)):
        for kept, v in zip((lows, highs), done):
            v = jnp.moveaxis(v, depth - 1, 0).reshape(group, slice_d, columns)
            kept.append((i * columns, v))
    gate_sum = join(lows, firsts, hidden_units)
    up_sum = join(highs, firsts, hidden_units)
    return (
        layer_out[None],
        grad_inputs[None],
        rest[:slice_d],
        joint[:slice_d, :qkv_width],
        rest[2 * slice_d : 2 * slice_d + slice_b],
        joint[:slice_d, qkv_width:],
        rest[slice_d : 2 * slice_d],
        gate_sum,
        up_sum,
        down_sum,
    )


def solution(mesh):
    return jax.shard_map(
        per_device,
        mesh=mesh,
        in_specs=(
            P("dp", "seq", None),
            P("dp", None),
            P("dp", "seq", None),
            P("seq"),
            P("seq", None),
            P("seq"),
            P("seq", None),
            P("seq"),
            P("seq", None),
            P("seq", None),
            P("seq", None),
        ),
        out_specs=(
            P("dp", "seq", None),
            P("dp", "seq", None),
            P("seq"),
            P("seq", None),
            P("seq"),
            P("seq", None),
            P("seq"),
            P("seq", None),
            P("seq", None),
            P("seq", None),
        ),
        check_vma=False,
    )
```
